1024 devices in a mesh: expert: 64 (over z, x), dp: 16 (over y, core).
Axes of the slice: x: 8, y: 8, z: 8, core: 2. Of those that a mesh axis runs over, the one named last changes fastest.
Arguments:
- expert_hidden: bfloat16 [192, 768, 1024], P('expert'), may hold values from -6 to 6
- down_weight: bfloat16 [128, 1024, 3584], P('expert', None, 'dp'), may hold values from -0.1875 to 0.1875
- out_grad: bfloat16 [6144, 3584], P('expert', 'dp'), may hold values from -6 to 6
- expert_ids: int32 [6144, 8], P('expert'), may hold values from 0 to 127, all different within a row; in each aligned block of 96 rows (0 to 95, 96 to 191, ...) at most 12 rows name the same one
- gate_code: int32 [6144, 8], P('expert'), may hold values from 0 to 15
- expert_load: int32 [128], replicated, may hold values from 0 to 999999
Outputs:
- mixed: bfloat16 [6144, 3584], P('expert', 'dp')
- hidden_grad: bfloat16 [192, 768, 1024], P('expert', 'dp')
- weight_grad: bfloat16 [128, 1024, 3584], P('expert', None, 'dp')
- spare_grad: bfloat16 [64, 1024, 3584], P('expert', None, 'dp')
The draws below stay inside these ranges and needn't reach their ends.
Inputs may be any that keep to these rules, and one draw needn't show every extreme that they name: `expert_ids`: each token's 8 picks are different experts; among the picks of the 96 tokens of one index of expert no expert appears more than 12 times, and in some such block an expert appears exactly 12 times.
All inputs are finite; a program needn't handle non-finite values.
Results may differ from the reference program's by a relative error of at most 0.022.
Values may be sent and summed in bfloat16 or wider, within the bound.
A program may use at most 64 MiB of HBM per device.

```python
import math
import jax
import jax.numpy as jnp
import numpy as np
from jax import lax

D = 3584
H = 1024
EXP_DEV = 2
TOP = 8
TOK_DEV = 96
EXPERTS = 128
TOKENS = 6144
SLOTS = 3
MOST = 12
N_EXPERT = 64
N_DP = 16


def touch_ends(entries, own_key, least, top_value):
    spot = [jax.random.randint(jax.random.fold_in(own_key, axis), (), 0, length) for axis, length in enumerate(entries.shape)]
    longest = entries.shape.index(max(entries.shape))
    next_to = spot[:longest] + [(spot[longest] + 1) % entries.shape[longest]] + spot[longest + 1:]
    return entries.at[tuple(spot)].set(least).at[tuple(next_to)].set(top_value)


def level_of(own_key, extent, split, low, high):
    loudness = 1.0
    for position, shards_of in split:
        heights = jax.random.uniform(jax.random.fold_in(jax.random.fold_in(own_key, 6), position), (shards_of,), jnp.float32, low / len(split), high / len(split))
        loudness = loudness * jnp.repeat(jnp.exp(heights), extent[position] // shards_of).reshape((-1,) + (1,) * (len(extent) - 1 - position))
    return loudness


def routed_block(key, own, number, rows, number_of, top, bound, slope):
    sequence = jax.random.permutation(key, number_of)
    heavy_load, usual = load_shares(number_of, rows * top, bound, slope, True), load_shares(number_of, rows * top, bound, slope, False)
    places = jnp.arange(number_of)

    def named(lengths, offset_by):
        used = int((lengths > 0).sum())
        fixed = max(1, used // 4)
        passed = fixed + (places - fixed + offset_by * (used - fixed)) % max(1, number_of - fixed)
        return jnp.zeros((number_of,), jnp.int32).at[sequence[jnp.where(places < fixed, places, passed)]].set(jnp.asarray(lengths, jnp.int32))

    lengths = jnp.where(number % 4 == 0, named(heavy_load, number // 4), named(usual, number - number // 4 - 1))
    mixed = jax.random.permutation(jax.random.fold_in(own, 3), number_of)
    giver, sink = mixed[0:number_of // 2 * 2:2], mixed[1:number_of // 2 * 2:2]
    margin = jnp.minimum(lengths[giver] - 1, bound - lengths[sink]) // 2
    margin = jnp.where((giver == sequence[0]) | (sink == sequence[0]) | (lengths[sink] == 0), 0, jnp.maximum(margin, 0))
    passed = jax.random.randint(jax.random.fold_in(own, 4), (number_of // 2,), 0, 1 << 20) % (margin + 1)
    lengths = lengths.at[giver].add(-passed).at[sink].add(passed)
    members = jnp.searchsorted(jnp.cumsum(lengths), jnp.arange(rows * top), side="right").astype(jnp.int32)
    table = members.reshape(top, rows).T
    table = table[jax.random.permutation(jax.random.fold_in(own, 1), rows)]
    offset_by = jax.random.randint(jax.random.fold_in(own, 2), (rows, 1), 0, top)
    return jnp.take_along_axis(table, (jnp.arange(top)[None, :] + offset_by) % top, axis=1)


def load_shares(number_of, total, most, skew, full):
    portions = [(1 << 20) // math.isqrt(grade ** skew) + 1 for grade in range(1, number_of + 1)]
    largest = most if full else min(most, max(-(-total // number_of), total * portions[0] // sum(portions)))
    least = 1 if total - largest >= number_of - 1 else 0
    given, surplus = [largest] + [least] * (number_of - 1), total - largest - least * (number_of - 1)
    while surplus > 0:
        free = [i for i in range(1, number_of) if given[i] < largest] or [i for i in range(1, number_of) if given[i] < most]
        pool, budget = sum([portions[i] for i in free]), surplus
        for i in free:
            more = min(most - given[i], max(1, budget * portions[i] // pool), surplus)
            given[i] = given[i] + more
            surplus = surplus - more
    return np.array(given)


def noise(key, shape, scale, most, pieces=(), kind=jnp.bfloat16):
    drawn = jax.random.normal(key, shape, jnp.float32) * scale
    if len(pieces) > 0:
        drawn = level_of(key, shape, pieces, -0.22, 0.18) * drawn
    return jnp.clip(drawn, min=-most, max=most).astype(kind)


def setup_inputs(seed: int = 0) -> dict:
    key_list = jax.random.split(jax.random.key(seed), 7)
    expert_hidden = noise(key_list[0], (N_EXPERT * SLOTS, N_EXPERT * MOST, H), 1.0, 6.0, ((0, 64),))
    down_weight = noise(key_list[1], (EXPERTS, H, D), H ** -0.5, 0.1875, ((0, 64), (2, 16)))
    out_grad = noise(key_list[2], (TOKENS, D), 1.0, 6.0, ((0, 64), (1, 16)))
    expert_ids_keys = jax.random.split(jax.random.fold_in(key_list[3], 1), TOKENS // TOK_DEV)
    expert_ids_turns = jax.random.permutation(jax.random.fold_in(key_list[3], 3), TOKENS // TOK_DEV)
    expert_ids = jax.vmap(lambda own, number: routed_block(jax.random.fold_in(key_list[3], 2), own, number, TOK_DEV, EXPERTS, TOP, MOST, 2))(expert_ids_keys, expert_ids_turns).reshape((TOKENS, TOP))
    gate_code = touch_ends(jax.random.randint(key_list[4], (TOKENS, TOP), 0, 16), jax.random.fold_in(key_list[4], 1), 0, 15).astype(jnp.int32)
    expert_load = touch_ends(jax.random.randint(key_list[5], (EXPERTS,), 0, 1000000), jax.random.fold_in(key_list[5], 1), 0, 999999).astype(jnp.int32)
    return {"expert_hidden": expert_hidden, "down_weight": down_weight, "out_grad": out_grad, "expert_ids": expert_ids, "gate_code": gate_code, "expert_load": expert_load}


def routing(expert_ids, expert_load):
    halfway = N_EXPERT // 2
    hottest = jnp.argmax(expert_load.reshape(N_EXPERT, EXP_DEV), axis=1).astype(jnp.int32)
    source = (jnp.arange(TOKENS, dtype=jnp.int32) // TOK_DEV)[:, None]
    home_dev = expert_ids // EXP_DEV
    home_slot = expert_ids % EXP_DEV
    spare_use = (home_slot == hottest[home_dev]) & (source // halfway != home_dev // halfway)
    target = jnp.where(spare_use, jnp.bitwise_xor(home_dev, halfway), home_dev)
    dest_slot = jnp.where(spare_use, EXP_DEV, home_slot)
    return target, dest_slot, hottest


def positions(slot_ids):
    labels = jnp.arange(N_EXPERT * SLOTS, dtype=jnp.int32)
    one_hot = (slot_ids[:, None] == labels[None, :]).astype(jnp.int32)
    before = jnp.cumsum(one_hot, axis=0) - one_hot
    return jnp.sum(before * one_hot, axis=1)


def reference(expert_hidden, down_weight, out_grad, expert_ids, gate_code, expert_load):
    halfway = N_EXPERT // 2
    target, dest_slot, hottest = routing(expert_ids, expert_load)
    slot_ids = (target * SLOTS + dest_slot).astype(jnp.int32)
    place = jax.vmap(positions)(slot_ids.reshape(N_EXPERT, TOK_DEV * TOP)).reshape(TOKENS, TOP)
    row_index = ((jnp.arange(TOKENS, dtype=jnp.int32) // TOK_DEV)[:, None] * MOST + place).astype(jnp.int32)
    gate_value = 0.0625 * (gate_code.astype(jnp.float32) + 1.0)
    slot_total = N_EXPERT * SLOTS
    row_total = N_EXPERT * MOST
    token_grid = jnp.broadcast_to(jnp.arange(TOKENS, dtype=jnp.int32)[:, None], (TOKENS, TOP))
    token_of = jnp.zeros((slot_total, row_total), jnp.int32).at[slot_ids, row_index].set(token_grid)
    weight_of = jnp.zeros((slot_total, row_total), jnp.float32).at[slot_ids, row_index].set(gate_value)
    slot_device = jnp.arange(slot_total, dtype=jnp.int32) // SLOTS
    slot_kind = jnp.arange(slot_total, dtype=jnp.int32) % SLOTS
    partner = jnp.bitwise_xor(slot_device, halfway)
    expert_of = jnp.where(slot_kind < EXP_DEV, slot_device * EXP_DEV + slot_kind,
                          partner * EXP_DEV + hottest[partner]).astype(jnp.int32)
    grad_scale = EXPERTS / TOKENS
    block_cols = D // N_DP

    def advance(mixed_sum, inputs):
        hidden, expert, token_rows, weights_here = inputs
        matrix = down_weight[expert].astype(jnp.float32)
        hidden_wide = hidden.astype(jnp.float32)
        outputs = jnp.dot(hidden_wide, matrix, preferred_element_type=jnp.float32).astype(jnp.bfloat16)
        mixed_sum = mixed_sum.at[token_rows].add(weights_here[:, None] * outputs.astype(jnp.float32))
        grad_rows = (weights_here[:, None] * out_grad[token_rows].astype(jnp.float32)).astype(jnp.bfloat16)
        grad_wide = grad_rows.astype(jnp.float32)
        grad_blocks = grad_wide.reshape(row_total, N_DP, block_cols)
        matrix_blocks = matrix.reshape(H, N_DP, block_cols)
        part_grad = jnp.einsum("rnc,hnc->nrh", grad_blocks, matrix_blocks, preferred_element_type=jnp.float32).astype(jnp.bfloat16)
        part_grad = lax.optimization_barrier(part_grad)
        hidden_back = jnp.sum(part_grad.astype(jnp.float32), axis=0).astype(jnp.bfloat16)
        matrix_grad = (grad_scale * jnp.dot(hidden_wide.T, grad_wide, preferred_element_type=jnp.float32)).astype(jnp.bfloat16)
        return mixed_sum, (hidden_back, matrix_grad)

    start = jnp.zeros((TOKENS, D), jnp.float32)
    mixed_sum, (hidden_grad, slot_grad) = lax.scan(advance, start, (expert_hidden, expert_of, token_of, weight_of))
    slot_grad = slot_grad.reshape(N_EXPERT, SLOTS, H, D)
    weight_grad = slot_grad[:, :EXP_DEV].reshape(EXPERTS, H, D)
    spare_grad = slot_grad[:, EXP_DEV]
    return mixed_sum.astype(jnp.bfloat16), hidden_grad, weight_grad, spare_grad
```

```python
import jax
import jax.numpy as jnp
from jax import lax
from jax.experimental import pallas as pl
from jax.experimental.pallas import tpu as pltpu
from jax.sharding import PartitionSpec as P

MESH = pl.DeviceIdType.MESH
BF = jnp.bfloat16
F32 = jnp.float32

Z = 8
X = 8
Y = 8
TOK = 96
LANES = 128
TOP = 8
MOST = 12
H = 1024
COLS = 224
HALF = 384
BLOCK = 48
RING = 7
SIDE = 512


def dot(a, b):
    return jnp.dot(a, b, preferred_element_type=F32)


def dot_nt(a, b):
    return lax.dot_general(a, b, (((1,), (1,)), ((), ())), preferred_element_type=F32)


def dot_tn(a, b):
    return lax.dot_general(a, b, (((0,), (0,)), ((), ())), preferred_element_type=F32)


def kernel(
    hid_hbm, w_hbm, og_ref, ids_ref, code_ref, load_ref,
    mixed_ref, hg_ref, wg_hbm, sg_hbm,
    hid, hid_n, hid_h, hid_c, w, w_n, w_h, w_c,
    turn, meta, tok, perm, perm_h,
    key_n, key_h, key_c, gate_n, gate_h, gate_c, g_n, g_hc,
    out_n, out_h, out_c, send_n, send_hc, recv_n, recv_hc,
    sb_n, sb_h, sb_c, back_n, back_hc, rg_n, rg_hc,
    cxs_n, cxs_h, cxs_c, cxr_n, cxr_h, cxr_c, sum_n, sum_h, sum_c,
    rs_n, rs_h, rs_c, rr_n, rr_h, rr_c,
    mix_s, mix_r, val_h, val_c, wg, sg,
    load_sem, zt_s, zt_r, zm_s, zm_r, wc_s, wc_r,
    dn_s, dn_r, dh_s, dh_r, bn_s, bn_r, bh_s, bh_r, bc_s, bc_r,
    cx_s, cx_r, ring_s, ring_r, mx_s, mx_r, out_sem,
):
    e = lax.axis_index("expert")
    dp = lax.axis_index("dp")
    z, x, y, c = e // X, e % X, dp // 2, dp % 2
    h = z // 4

    def z_peer(d):
        return (((z + d) % Z) * X + x, dp)

    def x_peer(d):
        return (z * X + (x + d) % X, dp)

    def y_peer(d):
        return (e, ((y + d) % Y) * 2 + c)

    sibling = (e, y * 2 + 1 - c)

    def remote(src, dst, s, r, to):
        return pltpu.make_async_remote_copy(
            src_ref=src, dst_ref=dst, send_sem=s, recv_sem=r, device_id=to, device_id_type=MESH
        )

    loads = [
        pltpu.make_async_copy(w_hbm, w, load_sem.at[0]),
        pltpu.make_async_copy(hid_hbm.at[0], hid.at[0], load_sem.at[1]),
        pltpu.make_async_copy(hid_hbm.at[1], hid.at[1], load_sem.at[2]),
        pltpu.make_async_copy(
            hid_hbm.at[2, pl.ds(pl.multiple_of(h * HALF, HALF), HALF)], hid_c, load_sem.at[3]
        ),
    ]
    for copy in loads:
        copy.start()

    barrier = pltpu.get_barrier_semaphore()
    peers = [z_peer(d) for d in range(1, Z)] + [x_peer(d) for d in range(1, X)]
    peers += [y_peer(1), y_peer(-1), sibling]
    for peer in peers:
        pl.semaphore_signal(barrier, inc=1, device_id=peer, device_id_type=MESH)

    turn[...] = jnp.full((LANES, LANES), -1.0, F32)
    turn[0:TOK, 0:TOP] = ids_ref[...].astype(F32)
    turn[0:TOK, TOP : 2 * TOP] = code_ref[...].astype(F32)
    meta[z] = turn[...].T[0 : 2 * TOP]
    tok[z, 0:TOK] = og_ref[...]
    for i in range(Z):
        tok[i, TOK:LANES] = jnp.zeros((LANES - TOK, COLS), BF)

    pl.semaphore_wait(barrier, len(peers))

    gather = []
    for i, d in enumerate((4, 3, -3, 2, -2, 1, -1)):
        gather.append(remote(meta.at[z], meta.at[z], zm_s.at[i], zm_r.at[i], z_peer(d)))
        gather.append(
            remote(tok.at[z, pl.ds(0, TOK)], tok.at[z, pl.ds(0, TOK)], zt_s.at[i], zt_r.at[i], z_peer(d))
        )
    for copy in gather:
        copy.start()

    own = load_ref[pl.ds(e, 1), :]
    hot = jnp.where(own[:, 1:2] > own[:, 0:1], 1.0, 0.0)
    hot_b, cold_b = hot.astype(BF), (1.0 - hot).astype(BF)
    cold = 1.0 - hot

    loads[0].wait()
    w_h[...] = w[0] * cold_b + w[1] * hot_b
    spare = remote(w_h, w_c, wc_s.at[0], wc_r.at[0], z_peer(4))
    spare.start()
    w_n[...] = w[0] * hot_b + w[1] * cold_b

    row = lax.broadcasted_iota(jnp.int32, (TOK, 1), 0)
    outer = jnp.zeros((TOK, 1), jnp.int32)
    for k in range(1, 8):
        outer = outer + jnp.where(row >= k * MOST, 1, 0)
    moved = outer * TOK + row - outer * MOST
    col = lax.broadcasted_iota(jnp.int32, (TOK, 2 * HALF), 1)
    for k in range(8):
        perm[k * TOK : (k + 1) * TOK] = jnp.where(col == moved + k * MOST, 1.0, 0.0).astype(BF)
    for k in range(8):
        perm_h[k * BLOCK : (k + 1) * BLOCK] = perm[k * TOK : k * TOK + BLOCK, 0:HALF]

    loads[1].wait()
    loads[2].wait()

    def forward_n(i, carry):
        at = pl.ds(pl.multiple_of(i * 256, 256), 256)
        rows = hid[0, at] * hot_b + hid[1, at] * cold_b
        hid_n[at] = rows
        out_n[at] = dot(rows, w_n[...]).astype(BF)
        return carry

    lax.fori_loop(0, 3, forward_n, 0)
    back = []
    for i in range(2):
        part = dot(perm[i * HALF : (i + 1) * HALF], out_n[...]).astype(BF)
        sb_n[4 * i : 4 * i + 4] = part.reshape(4, TOK, COLS)
    for i, d in enumerate((4, 3, -3, 2, -2, 1, -1)):
        copy = remote(sb_n.at[(x + d) % X], back_n.at[(-d) % X], bn_s.at[i], bn_r.at[i], x_peer(d))
        copy.start()
        back.append(copy)
    back_n[0] = sb_n[x]

    def forward_h(i, carry):
        at = pl.ds(pl.multiple_of(i * 128, 128), 128)
        far = pl.ds(pl.multiple_of(h * HALF + i * 128, 128), 128)
        rows = hid[0, far] * cold_b + hid[1, far] * hot_b
        hid_h[at] = rows
        out_h[at] = dot(rows, w_h[...]).astype(BF)
        return carry

    lax.fori_loop(0, 3, forward_h, 0)

    for copy in gather:
        copy.wait()

    def hottest(row_of_z):
        pair = load_ref[pl.ds(pl.multiple_of(row_of_z * X, X), X), :]
        return jnp.where(pair[:, 1:2] > pair[:, 0:1], 1.0, 0.0)

    at_x = lax.broadcasted_iota(jnp.int32, (X, 1), 0)
    far_z = (z + 4) % Z
    hot_here = hottest(z)
    home = (2 * (z * X + at_x)).astype(F32)
    name_n = home + 1.0 - hot_here
    name_h = home + hot_here
    name_c = (2 * (far_z * X + at_x)).astype(F32) + hottest(far_z)
    before = jnp.where(
        lax.broadcasted_iota(jnp.int32, (LANES, LANES), 0) < lax.broadcasted_iota(jnp.int32, (LANES, LANES), 1), 1.0, 0.0
    ).astype(BF)

    def match(facts, name):
        hits = jnp.zeros((X, LANES), F32)
        gates = jnp.zeros((X, LANES), F32)
        for k in range(TOP):
            same = facts[k : k + 1, :] == name
            hits = hits + jnp.where(same, 1.0, 0.0)
            gates = gates + jnp.where(same, 0.0625 * (facts[TOP + k : TOP + k + 1, :] + 1.0), 0.0)
        return hits, gates

    def keys(hits, first):
        places = dot(hits.astype(BF), before)
        return jnp.where(hits > 0.5, places + first, -1.0)

    for i in range(Z):
        hits, gates = match(meta[i], name_n)
        key_n[:, i * LANES : (i + 1) * LANES] = keys(hits, float(i * MOST))
        gate_n[:, i * LANES : (i + 1) * LANES] = gates
    for i in range(4):
        facts = meta[4 * h + i]
        hits, gates = match(facts, name_h)
        key_h[:, i * LANES : (i + 1) * LANES] = keys(hits, float(i * MOST))
        gate_h[:, i * LANES : (i + 1) * LANES] = gates
        hits, gates = match(facts, name_c)
        key_c[:, i * LANES : (i + 1) * LANES] = keys(hits, float(BLOCK + i * MOST))
        gate_c[:, i * LANES : (i + 1) * LANES] = gates

    order = (0, 4, 3, 5, 2, 6, 1, 7)
    places_n = lax.broadcasted_iota(jnp.int32, (TOK, Z * LANES), 0).astype(F32)
    dispatch_n = []
    for group in (order[0:4], order[4:8]):
        for d in group:
            at = pl.ds((x + d) % X, 1)
            i = order.index(d)
            g_n[i * TOK : (i + 1) * TOK] = jnp.where(key_n[at, :] == places_n, gate_n[at, :], 0.0).astype(BF)
        i = order.index(group[0])
        rows = dot(g_n[i * TOK : (i + 4) * TOK], tok[...].reshape(Z * LANES, COLS)).astype(BF)
        send_n[i : i + 4] = rows.reshape(4, TOK, COLS)
        for d in group:
            i = order.index(d)
            if d:
                copy = remote(send_n.at[i], recv_n.at[x], dn_s.at[i - 1], dn_r.at[i - 1], x_peer(d))
                copy.start()
                dispatch_n.append(copy)
            else:
                recv_n[x] = send_n[i]
    places_h = lax.broadcasted_iota(jnp.int32, (TOK, 4 * LANES), 0).astype(F32)
    dispatch_h = []
    for group in (order[0:4], order[4:8]):
        for d in group:
            at = pl.ds((x + d) % X, 1)
            i = order.index(d)
            g_hc[i * TOK : (i + 1) * TOK] = (
                jnp.where(key_h[at, :] == places_h, gate_h[at, :], 0.0)
                + jnp.where(key_c[at, :] == places_h, gate_c[at, :], 0.0)
            ).astype(BF)
        i = order.index(group[0])
        rows = dot(g_hc[i * TOK : (i + 4) * TOK], tok[pl.ds(4 * h, 4)].reshape(4 * LANES, COLS)).astype(BF)
        send_hc[i : i + 4] = rows.reshape(4, TOK, COLS)
        for d in group:
            i = order.index(d)
            if d:
                copy = remote(send_hc.at[i], recv_hc.at[x], dh_s.at[i - 1], dh_r.at[i - 1], x_peer(d))
                copy.start()
                dispatch_h.append(copy)
            else:
                recv_hc[x] = send_hc[i]

    part = dot(perm_h[...], out_h[...]).astype(BF)
    sb_h[...] = part.reshape(X, BLOCK, COLS)
    for i, d in enumerate((4, 3, -3, 2, -2, 1, -1)):
        copy = remote(
            sb_h.at[(x + d) % X], back_hc.at[order.index((-d) % X), pl.ds(0, BLOCK)], bh_s.at[i], bh_r.at[i], x_peer(d)
        )
        copy.start()
        back.append(copy)
    back_hc[0, 0:BLOCK] = sb_h[x]

    def partial(rg, first, count, weight, cxs, cxr, sums, sem):
        def rows_of(core):
            return jnp.concatenate(
                [
                    rg[pl.ds(pl.multiple_of(first + (2 * t + core) * BLOCK, 16), BLOCK), :]
                    for t in range(count)
                ],
                axis=0,
            )

        theirs = rows_of(1 - c)
        copies = []
        for side in range(2):
            part = dot_nt(theirs, weight[side * SIDE : (side + 1) * SIDE, :]).astype(BF)
            cxs[side] = part.reshape(count, BLOCK, SIDE)
            copy = remote(cxs.at[side], cxr.at[side], cx_s.at[sem + side], cx_r.at[sem + side], sibling)
            copy.start()
            copies.append(copy)
        mine = rows_of(c)
        for side in range(2):
            part = dot_nt(mine, weight[side * SIDE : (side + 1) * SIDE, :])
            sums[side] = part.reshape(count, BLOCK, SIDE)
        return copies

    for copy in dispatch_n:
        copy.wait()
    for i in range(2):
        rows = dot(perm[i * HALF : (i + 1) * HALF], recv_n[...].reshape(2 * HALF, COLS)).astype(BF)
        rg_n[i * HALF : (i + 1) * HALF] = rows
    pair_n = partial(rg_n, 0, 8, w_n, cxs_n, cxr_n, sum_n, 0)

    def at_step(side, k):
        return (y - (1 - 2 * side) * (1 + k)) % Y

    def ring_copy(kind, side, k):
        rs, rr = ((rs_n, rr_n), (rs_h, rr_h), (rs_c, rr_c))[kind]
        i = (kind * 2 + side) * RING + k
        return remote(rs.at[side, k], rr.at[side, k], ring_s.at[i], ring_r.at[i], y_peer(1 - 2 * side))

    def block_sum(kind, side, t, k):
        sums, cxr, rr = ((sum_n, cxr_n, rr_n), (sum_h, cxr_h, rr_h), (sum_c, cxr_c, rr_c))[kind]
        total = sums[side, t] + cxr[side, t].astype(F32)
        if k > 0:
            total = total + rr[side, k - 1].astype(F32)
        return total

    def ring_step(kind, k):
        rs = (rs_n, rs_h, rs_c)[kind]
        for side in range(2):
            t = at_step(side, k)

            def go(side=side, t=t):
                if k > 0:
                    ring_copy(kind, side, k - 1).wait_recv()
                rs[side, k] = block_sum(kind, side, t if kind == 0 else t % 4, k).astype(BF)
                ring_copy(kind, side, k).start()

            if kind == 0:
                go()
            else:
                pl.when(t // 4 == h)(go)

    def ring_end(kind):
        for side in range(2):
            for k in range(RING):
                if kind == 0:
                    ring_copy(kind, side, k).wait_send()
                else:

                    @pl.when(at_step(side, k) // 4 == h)
                    def _(side=side, k=k):
                        ring_copy(kind, side, k).wait_send()

    for copy in pair_n:
        copy.wait()
    ring_step(0, 0)

    for copy in dispatch_h:
        copy.wait()
    for i in range(2):
        rows = dot(perm[i * HALF : (i + 1) * HALF], recv_hc[...].reshape(2 * HALF, COLS)).astype(BF)
        rg_hc[i * HALF : (i + 1) * HALF] = rows
    pair_h = partial(rg_hc, 0, 4, w_h, cxs_h, cxr_h, sum_h, 2)
    ring_step(0, 1)
    for copy in pair_h:
        copy.wait()
    ring_step(1, 0)

    spare.wait()
    loads[3].wait()

    def forward_c(i, carry):
        at = pl.ds(pl.multiple_of(i * 128, 128), 128)
        out_c[at] = dot(hid_c[at], w_c[...]).astype(BF)
        return carry

    lax.fori_loop(0, 3, forward_c, 0)
    part = dot(perm_h[...], out_c[...]).astype(BF)
    sb_c[...] = part.reshape(X, BLOCK, COLS)
    for i, d in enumerate((4, 3, -3, 2, -2, 1, -1)):
        copy = remote(
            sb_c.at[(x + d) % X], back_hc.at[order.index((-d) % X), pl.ds(BLOCK, BLOCK)], bc_s.at[i], bc_r.at[i], x_peer(d)
        )
        copy.start()
        back.append(copy)
    back_hc[0, BLOCK:TOK] = sb_c[x]
    pair_c = partial(rg_hc, HALF, 4, w_c, cxs_c, cxr_c, sum_c, 4)
    ring_step(0, 2)
    ring_step(1, 1)
    for copy in pair_c:
        copy.wait()
    ring_step(2, 0)

    scale = 2.0 / TOK

    def weight_part(i):
        at = slice(i * 256, (i + 1) * 256)
        grad_n = scale * dot_tn(hid_n[:, at], rg_n[...])
        grad_h = scale * dot_tn(hid_h[:, at], rg_hc[0:HALF])
        wg[0, at] = (grad_n * hot + grad_h * cold).astype(BF)
        wg[1, at] = (grad_n * cold + grad_h * hot).astype(BF)
        sg[0, at] = (scale * dot_tn(hid_c[:, at], rg_hc[HALF : 2 * HALF])).astype(BF)

    for k in range(4):
        ring_step(0, 3 + k)
        ring_step(1, 2 + k)
        ring_step(2, 1 + k)
        weight_part(k)
    stores = [
        pltpu.make_async_copy(wg, wg_hbm, out_sem.at[0]),
        pltpu.make_async_copy(sg, sg_hbm, out_sem.at[1]),
    ]
    for copy in stores:
        copy.start()

    for copy in back:
        copy.wait()
    ring_step(1, 6)
    ring_step(2, 5)

    def combine(i):
        at = slice(i * LANES, (i + 1) * LANES)
        return dot_tn(g_n[:, at], back_n_rows())

    def back_n_rows():
        return jnp.concatenate([back_n[d] for d in order], axis=0)

    total = dot_tn(g_n[...], back_n_rows()).reshape(Z, LANES, COLS)
    mix_s[...] = total[:, 0:TOK]
    near = dot_tn(g_hc[...], back_hc[...].reshape(X * TOK, COLS)).reshape(4, LANES, COLS)
    mix_s[pl.ds(4 * h, 4)] = mix_s[pl.ds(4 * h, 4)] + near[:, 0:TOK]
    mix = []
    for i, d in enumerate((4, 3, -3, 2, -2, 1, -1)):
        mix_r[8 + i] = mix_s[(z + d) % Z].astype(BF)
        copy = remote(mix_r.at[8 + i], mix_r.at[i], mx_s.at[i], mx_r.at[i], z_peer(d))
        copy.start()
        mix.append(copy)
    ring_step(2, 6)

    val_h[...] = jnp.zeros_like(val_h)
    val_c[...] = jnp.zeros_like(val_c)
    value_n = []
    for side in range(2):
        ring_copy(0, side, RING - 1).wait_recv()
        value_n.append(block_sum(0, side, y, RING))

    @pl.when(y // 4 == h)
    def _():
        for side in range(2):
            at = slice(side * SIDE, (side + 1) * SIDE)
            ring_copy(1, side, RING - 1).wait_recv()
            val_h[:, at] = block_sum(1, side, y % 4, RING)
            ring_copy(2, side, RING - 1).wait_recv()
            val_c[:, at] = block_sum(2, side, y % 4, RING)

    for side in range(2):
        at = slice(side * SIDE, (side + 1) * SIDE)
        hg_ref[0, :, at] = (value_n[side] * hot + val_h[:, at] * cold).astype(BF)
        hg_ref[1, :, at] = (value_n[side] * cold + val_h[:, at] * hot).astype(BF)
    hg_ref[2] = val_c[...].astype(BF)

    total = mix_s[z].astype(BF).astype(F32)
    for copy in mix:
        copy.wait()
    for i in range(Z - 1):
        total = total + mix_r[i].astype(F32)
    mixed_ref[...] = total.astype(BF)

    for kind in range(3):
        ring_end(kind)
    for copy in stores:
        copy.wait()


def body(expert_hidden, down_weight, out_grad, expert_ids, gate_code, expert_load):
    vmem = pl.BlockSpec(memory_space=pltpu.VMEM)
    anywhere = pl.BlockSpec(memory_space=pl.ANY)
    dma = pltpu.SemaphoreType.DMA

    def b(*shape):
        return pltpu.VMEM(shape, BF)

    def f(*shape):
        return pltpu.VMEM(shape, F32)

    scratch = [
        b(2, 2 * HALF, H), b(2 * HALF, H), b(HALF, H), b(HALF, H),
        b(2, H, COLS), b(H, COLS), b(H, COLS), b(H, COLS),
        f(LANES, LANES), f(Z, 2 * TOP, LANES), b(Z, LANES, COLS), b(2 * HALF, 2 * HALF), b(HALF, HALF),
        f(X, Z * LANES), f(X, 4 * LANES), f(X, 4 * LANES), f(X, Z * LANES), f(X, 4 * LANES), f(X, 4 * LANES),
        b(X * TOK, Z * LANES), b(X * TOK, 4 * LANES),
        b(2 * HALF, COLS), b(HALF, COLS), b(HALF, COLS),
        b(X, TOK, COLS), b(X, TOK, COLS), b(X, TOK, COLS), b(X, TOK, COLS),
        b(X, TOK, COLS), b(X, BLOCK, COLS), b(X, BLOCK, COLS), b(X, TOK, COLS), b(X, TOK, COLS),
        b(2 * HALF, COLS), b(2 * HALF, COLS),
        b(2, 8, BLOCK, SIDE), b(2, 4, BLOCK, SIDE), b(2, 4, BLOCK, SIDE),
        b(2, 8, BLOCK, SIDE), b(2, 4, BLOCK, SIDE), b(2, 4, BLOCK, SIDE),
        f(2, 8, BLOCK, SIDE), f(2, 4, BLOCK, SIDE), f(2, 4, BLOCK, SIDE),
        b(2, RING, BLOCK, SIDE), b(2, RING, BLOCK, SIDE), b(2, RING, BLOCK, SIDE),
        b(2, RING, BLOCK, SIDE), b(2, RING, BLOCK, SIDE), b(2, RING, BLOCK, SIDE),
        f(Z, TOK, COLS), b(2 * Z, TOK, COLS), f(BLOCK, H), f(BLOCK, H), b(2, H, COLS), b(1, H, COLS),
        dma((4,)), dma((7,)), dma((7,)), dma((7,)), dma((7,)), dma((1,)), dma((1,)),
        dma((7,)), dma((7,)), dma((7,)), dma((7,)), dma((7,)), dma((7,)), dma((7,)), dma((7,)), dma((7,)), dma((7,)),
        dma((6,)), dma((6,)), dma((6 * RING,)), dma((6 * RING,)), dma((7,)), dma((7,)), dma((2,)),
    ]
    return pl.pallas_call(
        kernel,
        out_shape=(
            jax.ShapeDtypeStruct((TOK, COLS), BF),
            jax.ShapeDtypeStruct((3, BLOCK, H), BF),
            jax.ShapeDtypeStruct((2, H, COLS), BF),
            jax.ShapeDtypeStruct((1, H, COLS), BF),
        ),
        in_specs=[anywhere, anywhere, vmem, vmem, vmem, vmem],
        out_specs=(vmem, vmem, anywhere, anywhere),
        scratch_shapes=scratch,
        compiler_params=pltpu.CompilerParams(
            collective_id=0, has_side_effects=True, vmem_limit_bytes=58 * 1024 * 1024
        ),
        name="experts",
    )(expert_hidden, down_weight, out_grad, expert_ids, gate_code, expert_load.reshape(64, 2))


def solution(mesh):
    placed = (
        P("expert", None, None),
        P("expert", None, "dp"),
        P("expert", "dp"),
        P("expert", None),
        P("expert", None),
        P(),
    )
    return jax.shard_map(
        body,
        mesh=mesh,
        in_specs=placed,
        out_specs=(
            P("expert", "dp"),
            P("expert", "dp", None),
            P("expert", None, "dp"),
            P("expert", None, "dp"),
        ),
        check_vma=False,
    )
```

```python
import jax
import jax.numpy as jnp
from jax import lax
from jax.experimental import pallas as pl
from jax.experimental.pallas import tpu as pltpu
from jax.sharding import PartitionSpec as P

MESH = pl.DeviceIdType.MESH
BF = jnp.bfloat16
F32 = jnp.float32

Z = 8
X = 8
Y = 8
TOK = 96
LANES = 128
TOP = 8
MOST = 12
H = 1024
COLS = 224
HALF = 384
BLOCK = 48
RING = 7
SIDE = 512


def dot(a, b):
    return jnp.dot(a, b, preferred_element_type=F32)


def dot_nt(a, b):
    return lax.dot_general(a, b, (((1,), (1,)), ((), ())), preferred_element_type=F32)


def dot_tn(a, b):
    return lax.dot_general(a, b, (((0,), (0,)), ((), ())), preferred_element_type=F32)


def kernel(
    hid_hbm, w_hbm, og_ref, ids_ref, code_ref, load_ref,
    mixed_ref, hg_ref, wg_hbm, sg_hbm,
    hid, hid_n, hid_h, hid_c, w, w_n, w_h, w_c,
    meta, tok, perm, perm_h,
    key_n, key_h, key_c, gate_n, gate_h, gate_c, g_n, g_hc, gt_n, gt_hc,
    out_n, out_h, out_c, send_n, send_hc, recv_n, recv_hc,
    sb_n, sb_h, sb_c, back_n, back_hc, rg_n, rg_hc, rgt_n, rgt_hc,
    cxs_n, cxs_h, cxs_c, cxr_n, cxr_h, cxr_c, sum_n, sum_h, sum_c,
    rs_n, rs_h, rs_c, rr_n, rr_h, rr_c,
    mix_s, mix_r, val_h, val_c, wg, sg,
    load_sem, zt_s, zt_r, zm_s, zm_r, wc_s, wc_r,
    dn_s, dn_r, dh_s, dh_r, bn_s, bn_r, bh_s, bh_r, bc_s, bc_r,
    cx_s, cx_r, ring_s, ring_r, mx_s, mx_r, out_sem,
):
    e = lax.axis_index("expert")
    dp = lax.axis_index("dp")
    z, x, y, c = e // X, e % X, dp // 2, dp % 2
    h = z // 4

    def z_peer(d):
        return (((z + d) % Z) * X + x, dp)

    def x_peer(d):
        return (z * X + (x + d) % X, dp)

    def y_peer(d):
        return (e, ((y + d) % Y) * 2 + c)

    sibling = (e, y * 2 + 1 - c)

    def remote(src, dst, s, r, to):
        return pltpu.make_async_remote_copy(
            src_ref=src, dst_ref=dst, send_sem=s, recv_sem=r, device_id=to, device_id_type=MESH
        )

    loads = [
        pltpu.make_async_copy(w_hbm, w, load_sem.at[0]),
        pltpu.make_async_copy(hid_hbm.at[0], hid.at[0], load_sem.at[1]),
        pltpu.make_async_copy(hid_hbm.at[1], hid.at[1], load_sem.at[2]),
        pltpu.make_async_copy(
            hid_hbm.at[2, pl.ds(pl.multiple_of(h * HALF, HALF), HALF)], hid_c, load_sem.at[3]
        ),
    ]
    for copy in loads:
        copy.start()

    barrier = pltpu.get_barrier_semaphore()
    peers = [z_peer(d) for d in range(1, Z)] + [x_peer(d) for d in range(1, X)]
    peers += [y_peer(1), y_peer(-1), sibling]
    for peer in peers:
        pl.semaphore_signal(barrier, inc=1, device_id=peer, device_id_type=MESH)

    meta[z] = jnp.full((2 * TOP, LANES), -1.0, BF)
    facts = jnp.concatenate([ids_ref[...].astype(F32), code_ref[...].astype(F32)], axis=0)
    meta[z, :, 0:TOK] = facts.astype(BF)
    tok[z, 0:TOK] = og_ref[...]
    for i in range(Z):
        tok[i, TOK:LANES] = jnp.zeros((LANES - TOK, COLS), BF)

    pl.semaphore_wait(barrier, len(peers))

    gather = []
    for i, d in enumerate((4, 3, -3, 2, -2, 1, -1)):
        gather.append(remote(meta.at[z], meta.at[z], zm_s.at[i], zm_r.at[i], z_peer(d)))
        gather.append(
            remote(tok.at[z, pl.ds(0, TOK)], tok.at[z, pl.ds(0, TOK)], zt_s.at[i], zt_r.at[i], z_peer(d))
        )
    for copy in gather:
        copy.start()

    lane = lax.broadcasted_iota(jnp.int32, (X, LANES), 1)
    at_x = lax.broadcasted_iota(jnp.int32, (X, 1), 0)
    loads_all = jnp.broadcast_to(load_ref[...].astype(F32), (X, LANES))

    def hottest(row_of_z):
        first = 2 * (row_of_z * X + at_x)
        even = jnp.sum(jnp.where(lane == first, loads_all, 0.0), axis=1, keepdims=True)
        odd = jnp.sum(jnp.where(lane == first + 1, loads_all, 0.0), axis=1, keepdims=True)
        return jnp.where(odd > even, 1.0, 0.0)

    hot_here = hottest(z)
    hot = jnp.sum(jnp.where(at_x == x, hot_here, 0.0), axis=0, keepdims=True)
    hot_b, cold_b = hot.astype(BF), (1.0 - hot).astype(BF)
    cold = 1.0 - hot

    loads[0].wait()
    w_h[...] = w[0] * cold_b + w[1] * hot_b
    w_n[...] = w[0] * hot_b + w[1] * cold_b

    row = lax.broadcasted_iota(jnp.int32, (TOK, 1), 0)
    outer = jnp.zeros((TOK, 1), jnp.int32)
    for k in range(1, 8):
        outer = outer + jnp.where(row >= k * MOST, 1, 0)
    moved = outer * TOK + row - outer * MOST
    col = lax.broadcasted_iota(jnp.int32, (TOK, 2 * HALF), 1)
    for k in range(8):
        perm[k * TOK : (k + 1) * TOK] = jnp.where(col == moved + k * MOST, 1.0, 0.0).astype(BF)
    for k in range(8):
        perm_h[k * BLOCK : (k + 1) * BLOCK] = perm[k * TOK : k * TOK + BLOCK, 0:HALF]

    loads[1].wait()
    loads[2].wait()

    def forward_n(i, carry):
        at = pl.ds(pl.multiple_of(i * 256, 256), 256)
        rows = hid[0, at] * hot_b + hid[1, at] * cold_b
        hid_n[at] = rows
        out_n[at] = dot_nt(rows, w_n[...]).astype(BF)
        return carry

    lax.fori_loop(0, 3, forward_n, 0)
    back = []
    for i in range(2):
        part = dot(perm[i * HALF : (i + 1) * HALF], out_n[...]).astype(BF)
        sb_n[4 * i : 4 * i + 4] = part.reshape(4, TOK, COLS)
    for i, d in enumerate((4, 3, -3, 2, -2, 1, -1)):
        copy = remote(sb_n.at[(x + d) % X], back_n.at[(-d) % X], bn_s.at[i], bn_r.at[i], x_peer(d))
        copy.start()
        back.append(copy)
    back_n[0] = sb_n[x]

    for copy in gather:
        copy.wait()
    spare = remote(w_h, w_c, wc_s.at[0], wc_r.at[0], z_peer(4))
    spare.start()

    far_z = (z + 4) % Z
    home = (2 * (z * X + at_x)).astype(F32)
    name_n = home + 1.0 - hot_here
    name_h = home + hot_here
    name_c = (2 * (far_z * X + at_x)).astype(F32) + hottest(far_z)
    before = jnp.where(
        lax.broadcasted_iota(jnp.int32, (LANES, LANES), 0) < lax.broadcasted_iota(jnp.int32, (LANES, LANES), 1), 1.0, 0.0
    ).astype(BF)

    def match(facts, name):
        hits = jnp.zeros((X, LANES), F32)
        gates = jnp.zeros((X, LANES), F32)
        for k in range(TOP):
            same = facts[k : k + 1, :] == name
            hits = hits + jnp.where(same, 1.0, 0.0)
            gates = gates + jnp.where(same, 0.0625 * (facts[TOP + k : TOP + k + 1, :] + 1.0), 0.0)
        return hits, gates

    def keys(hits, first):
        places = dot(hits.astype(BF), before)
        return jnp.where(hits > 0.5, places + first, -1.0)

    for i in range(Z):
        hits, gates = match(meta[i].astype(F32), name_n)
        key_n[:, i * LANES : (i + 1) * LANES] = keys(hits, float(i * MOST))
        gate_n[:, i * LANES : (i + 1) * LANES] = gates
    for i in range(4):
        facts = meta[4 * h + i].astype(F32)
        hits, gates = match(facts, name_h)
        key_h[:, i * LANES : (i + 1) * LANES] = keys(hits, float(i * MOST))
        gate_h[:, i * LANES : (i + 1) * LANES] = gates
        hits, gates = match(facts, name_c)
        key_c[:, i * LANES : (i + 1) * LANES] = keys(hits, float(BLOCK + i * MOST))
        gate_c[:, i * LANES : (i + 1) * LANES] = gates

    order = (0, 4, 3, 5, 2, 6, 1, 7)
    places_n = lax.broadcasted_iota(jnp.int32, (TOK, Z * LANES), 0).astype(F32)
    dispatch_n = []
    for group in (order[0:4], order[4:8]):
        for d in group:
            at = pl.ds((x + d) % X, 1)
            i = order.index(d)
            g_n[i * TOK : (i + 1) * TOK] = jnp.where(key_n[at, :] == places_n, gate_n[at, :], 0.0).astype(BF)
        i = order.index(group[0])
        rows = dot(g_n[i * TOK : (i + 4) * TOK], tok[...].reshape(Z * LANES, COLS)).astype(BF)
        send_n[i : i + 4] = rows.reshape(4, TOK, COLS)
        for d in group:
            i = order.index(d)
            if d:
                copy = remote(send_n.at[i], recv_n.at[x], dn_s.at[i - 1], dn_r.at[i - 1], x_peer(d))
                copy.start()
                dispatch_n.append(copy)
            else:
                recv_n[x] = send_n[i]
    places_h = lax.broadcasted_iota(jnp.int32, (TOK, 4 * LANES), 0).astype(F32)
    dispatch_h = []
    for group in (order[0:4], order[4:8]):
        for d in group:
            at = pl.ds((x + d) % X, 1)
            i = order.index(d)
            g_hc[i * TOK : (i + 1) * TOK] = (
                jnp.where(key_h[at, :] == places_h, gate_h[at, :], 0.0)
                + jnp.where(key_c[at, :] == places_h, gate_c[at, :], 0.0)
            ).astype(BF)
        i = order.index(group[0])
        rows = dot(g_hc[i * TOK : (i + 4) * TOK], tok[pl.ds(4 * h, 4)].reshape(4 * LANES, COLS)).astype(BF)
        send_hc[i : i + 4] = rows.reshape(4, TOK, COLS)
        for d in group:
            i = order.index(d)
            if d:
                copy = remote(send_hc.at[i], recv_hc.at[x], dh_s.at[i - 1], dh_r.at[i - 1], x_peer(d))
                copy.start()
                dispatch_h.append(copy)
            else:
                recv_hc[x] = send_hc[i]

    def forward_h(i, carry):
        at = pl.ds(pl.multiple_of(i * 128, 128), 128)
        far = pl.ds(pl.multiple_of(h * HALF + i * 128, 128), 128)
        rows = hid[0, far] * cold_b + hid[1, far] * hot_b
        hid_h[at] = rows
        out_h[at] = dot_nt(rows, w_h[...]).astype(BF)
        return carry

    lax.fori_loop(0, 3, forward_h, 0)

    part = dot(perm_h[...], out_h[...]).astype(BF)
    sb_h[...] = part.reshape(X, BLOCK, COLS)
    for i in range(4):
        at = slice(i * 2 * LANES, (i + 1) * 2 * LANES)
        gt_n[at] = g_n[:, at].T
    for i in range(2):
        at = slice(i * 2 * LANES, (i + 1) * 2 * LANES)
        gt_hc[at] = g_hc[:, at].T

    def partial(rg, first, count, weight, cxs, cxr, sums, sem):
        def rows_of(core):
            return jnp.concatenate(
                [
                    rg[pl.ds(pl.multiple_of(first + (2 * t + core) * BLOCK, 16), BLOCK), :]
                    for t in range(count)
                ],
                axis=0,
            )

        theirs = rows_of(1 - c)
        copies = []
        for side in range(2):
            part = dot(theirs, weight[:, side * SIDE : (side + 1) * SIDE]).astype(BF)
            cxs[side] = part.reshape(count, BLOCK, SIDE)
            copy = remote(cxs.at[side], cxr.at[side], cx_s.at[sem + side], cx_r.at[sem + side], sibling)
            copy.start()
            copies.append(copy)
        mine = rows_of(c)
        for side in range(2):
            part = dot(mine, weight[:, side * SIDE : (side + 1) * SIDE])
            sums[side] = part.reshape(count, BLOCK, SIDE)
        return copies

    for copy in dispatch_n:
        copy.wait()
    for i in range(2):
        rows = dot(perm[i * HALF : (i + 1) * HALF], recv_n[...].reshape(2 * HALF, COLS)).astype(BF)
        rg_n[i * HALF : (i + 1) * HALF] = rows
    pair_n = partial(rg_n, 0, 8, w_n, cxs_n, cxr_n, sum_n, 0)

    def at_step(side, k):
        return (y - (1 - 2 * side) * (1 + k)) % Y

    def ring_copy(kind, side, k):
        rs, rr = ((rs_n, rr_n), (rs_h, rr_h), (rs_c, rr_c))[kind]
        i = (kind * 2 + side) * RING + k
        return remote(rs.at[side, k], rr.at[side, k], ring_s.at[i], ring_r.at[i], y_peer(1 - 2 * side))

    def block_sum(kind, side, t, k):
        sums, cxr, rr = ((sum_n, cxr_n, rr_n), (sum_h, cxr_h, rr_h), (sum_c, cxr_c, rr_c))[kind]
        total = sums[side, t] + cxr[side, t].astype(F32)
        if k > 0:
            total = total + rr[side, k - 1].astype(F32)
        return total

    def ring_step(kind, k):
        rs = (rs_n, rs_h, rs_c)[kind]
        for side in range(2):
            t = at_step(side, k)

            def go(side=side, t=t):
                if k > 0:
                    ring_copy(kind, side, k - 1).wait_recv()
                rs[side, k] = block_sum(kind, side, t if kind == 0 else t % 4, k).astype(BF)
                ring_copy(kind, side, k).start()

            if kind == 0:
                go()
            else:
                pl.when(t // 4 == h)(go)

    def ring_end(kind):
        for side in range(2):
            for k in range(RING):
                if kind == 0:
                    ring_copy(kind, side, k).wait_send()
                else:

                    @pl.when(at_step(side, k) // 4 == h)
                    def _(side=side, k=k):
                        ring_copy(kind, side, k).wait_send()

    for i, d in enumerate((4, 3, -3, 2, -2, 1, -1)):
        copy = remote(
            sb_h.at[(x + d) % X], back_hc.at[order.index((-d) % X), pl.ds(0, BLOCK)], bh_s.at[i], bh_r.at[i], x_peer(d)
        )
        copy.start()
        back.append(copy)
    back_hc[0, 0:BLOCK] = sb_h[x]

    for copy in pair_n:
        copy.wait()
    ring_step(0, 0)
    ring_step(0, 1)

    for copy in dispatch_h:
        copy.wait()
    for i in range(2):
        rows = dot(perm[i * HALF : (i + 1) * HALF], recv_hc[...].reshape(2 * HALF, COLS)).astype(BF)
        rg_hc[i * HALF : (i + 1) * HALF] = rows
    pair_h = partial(rg_hc, 0, 4, w_h, cxs_h, cxr_h, sum_h, 2)
    ring_step(0, 2)
    for copy in pair_h:
        copy.wait()
    ring_step(1, 0)
    ring_step(0, 3)
    ring_step(1, 1)

    spare.wait()
    loads[3].wait()

    def forward_c(i, carry):
        at = pl.ds(pl.multiple_of(i * 128, 128), 128)
        out_c[at] = dot_nt(hid_c[at], w_c[...]).astype(BF)
        return carry

    lax.fori_loop(0, 3, forward_c, 0)
    part = dot(perm_h[...], out_c[...]).astype(BF)
    sb_c[...] = part.reshape(X, BLOCK, COLS)
    for i, d in enumerate((4, 3, -3, 2, -2, 1, -1)):
        copy = remote(
            sb_c.at[(x + d) % X], back_hc.at[order.index((-d) % X), pl.ds(BLOCK, BLOCK)], bc_s.at[i], bc_r.at[i], x_peer(d)
        )
        copy.start()
        back.append(copy)
    back_hc[0, BLOCK:TOK] = sb_c[x]
    pair_c = partial(rg_hc, HALF, 4, w_c, cxs_c, cxr_c, sum_c, 4)
    ring_step(0, 4)
    ring_step(1, 2)
    for copy in pair_c:
        copy.wait()
    ring_step(2, 0)

    scale = 2.0 / TOK

    def turn_rows():
        rgt_n[...] = rg_n[...].T
        rgt_hc[...] = rg_hc[...].T

    def weight_part(i):
        at = slice(i * SIDE, (i + 1) * SIDE)
        grad_n = scale * dot(rgt_n[...], hid_n[:, at])
        grad_h = scale * dot(rgt_hc[:, 0:HALF], hid_h[:, at])
        wg[0, :, at] = (grad_n * hot + grad_h * cold).astype(BF)
        wg[1, :, at] = (grad_n * cold + grad_h * hot).astype(BF)
        sg[0, :, at] = (scale * dot(rgt_hc[:, HALF : 2 * HALF], hid_c[:, at])).astype(BF)

    turn_rows()
    ring_step(0, 5)
    ring_step(1, 3)
    ring_step(2, 1)
    for copy in back[0:7]:
        copy.wait()
    rows = jnp.concatenate([back_n[d] for d in order], axis=0)
    mix_s[...] = dot(gt_n[...], rows).reshape(Z, LANES, COLS)[:, 0:TOK]
    ring_step(0, 6)
    ring_step(1, 4)
    ring_step(2, 2)
    for copy in back[7:]:
        copy.wait()
    near = dot(gt_hc[...], back_hc[...].reshape(X * TOK, COLS)).reshape(4, LANES, COLS)
    mix_s[pl.ds(4 * h, 4)] = mix_s[pl.ds(4 * h, 4)] + near[:, 0:TOK]
    mix = []
    for i, d in enumerate((4, 3, -3, 2, -2, 1, -1)):
        mix_r[8 + i] = mix_s[(z + d) % Z].astype(BF)
        copy = remote(mix_r.at[8 + i], mix_r.at[i], mx_s.at[i], mx_r.at[i], z_peer(d))
        copy.start()
        mix.append(copy)
    ring_step(1, 5)
    ring_step(2, 3)
    weight_part(0)
    ring_step(1, 6)
    ring_step(2, 4)
    weight_part(1)
    stores = [
        pltpu.make_async_copy(wg, wg_hbm, out_sem.at[0]),
        pltpu.make_async_copy(sg, sg_hbm, out_sem.at[1]),
    ]
    for copy in stores:
        copy.start()
    ring_step(2, 5)
    ring_step(2, 6)

    val_h[...] = jnp.zeros_like(val_h)
    val_c[...] = jnp.zeros_like(val_c)
    value_n = []
    for side in range(2):
        ring_copy(0, side, RING - 1).wait_recv()
        value_n.append(block_sum(0, side, y, RING))

    @pl.when(y // 4 == h)
    def _():
        for side in range(2):
            at = slice(side * SIDE, (side + 1) * SIDE)
            ring_copy(1, side, RING - 1).wait_recv()
            val_h[:, at] = block_sum(1, side, y % 4, RING)
            ring_copy(2, side, RING - 1).wait_recv()
            val_c[:, at] = block_sum(2, side, y % 4, RING)

    for side in range(2):
        at = slice(side * SIDE, (side + 1) * SIDE)
        hg_ref[0, :, at] = (value_n[side] * hot + val_h[:, at] * cold).astype(BF)
        hg_ref[1, :, at] = (value_n[side] * cold + val_h[:, at] * hot).astype(BF)
    hg_ref[2] = val_c[...].astype(BF)

    total = mix_s[z]
    for copy in mix:
        copy.wait()
    for i in range(Z - 1):
        total = total + mix_r[i].astype(F32)
    mixed_ref[...] = total.astype(BF)

    for kind in range(3):
        ring_end(kind)
    for copy in stores:
        copy.wait()


def store(*refs):
    sem = refs[8]
    copies = [pltpu.make_async_copy(refs[i], refs[4 + i], sem.at[i]) for i in range(4)]
    for copy in copies:
        copy.start()
    for copy in copies:
        copy.wait()


def body(expert_hidden, down_weight, out_grad, expert_ids, gate_code, expert_load):
    vmem = pl.BlockSpec(memory_space=pltpu.VMEM)
    anywhere = pl.BlockSpec(memory_space=pl.ANY)
    dma = pltpu.SemaphoreType.DMA

    def b(*shape):
        return pltpu.VMEM(shape, BF)

    def f(*shape):
        return pltpu.VMEM(shape, F32)

    scratch = [
        b(2, 2 * HALF, H), b(2 * HALF, H), b(HALF, H), b(HALF, H),
        b(2, COLS, H), b(COLS, H), b(COLS, H), b(COLS, H),
        b(Z, 2 * TOP, LANES), b(Z, LANES, COLS), b(2 * HALF, 2 * HALF), b(HALF, HALF),
        f(X, Z * LANES), f(X, 4 * LANES), f(X, 4 * LANES), f(X, Z * LANES), f(X, 4 * LANES), f(X, 4 * LANES),
        b(X * TOK, Z * LANES), b(X * TOK, 4 * LANES), b(Z * LANES, X * TOK), b(4 * LANES, X * TOK),
        b(2 * HALF, COLS), b(HALF, COLS), b(HALF, COLS),
        b(X, TOK, COLS), b(X, TOK, COLS), b(X, TOK, COLS), b(X, TOK, COLS),
        b(X, TOK, COLS), b(X, BLOCK, COLS), b(X, BLOCK, COLS), b(X, TOK, COLS), b(X, TOK, COLS),
        b(2 * HALF, COLS), b(2 * HALF, COLS), b(COLS, 2 * HALF), b(COLS, 2 * HALF),
        b(2, 8, BLOCK, SIDE), b(2, 4, BLOCK, SIDE), b(2, 4, BLOCK, SIDE),
        b(2, 8, BLOCK, SIDE), b(2, 4, BLOCK, SIDE), b(2, 4, BLOCK, SIDE),
        f(2, 8, BLOCK, SIDE), f(2, 4, BLOCK, SIDE), f(2, 4, BLOCK, SIDE),
        b(2, RING, BLOCK, SIDE), b(2, RING, BLOCK, SIDE), b(2, RING, BLOCK, SIDE),
        b(2, RING, BLOCK, SIDE), b(2, RING, BLOCK, SIDE), b(2, RING, BLOCK, SIDE),
        f(Z, TOK, COLS), b(2 * Z, TOK, COLS), f(BLOCK, H), f(BLOCK, H), b(2, COLS, H), b(1, COLS, H),
        dma((4,)), dma((7,)), dma((7,)), dma((7,)), dma((7,)), dma((1,)), dma((1,)),
        dma((7,)), dma((7,)), dma((7,)), dma((7,)), dma((7,)), dma((7,)), dma((7,)), dma((7,)), dma((7,)), dma((7,)),
        dma((6,)), dma((6,)), dma((6 * RING,)), dma((6 * RING,)), dma((7,)), dma((7,)), dma((2,)),
    ]
    shapes = (
        jax.ShapeDtypeStruct((TOK, COLS), BF),
        jax.ShapeDtypeStruct((3, BLOCK, H), BF),
        jax.ShapeDtypeStruct((2, COLS, H), BF),
        jax.ShapeDtypeStruct((1, COLS, H), BF),
    )
    results = pl.pallas_call(
        kernel,
        out_shape=shapes,
        in_specs=[anywhere, anywhere, vmem, vmem, vmem, vmem],
        out_specs=(vmem, vmem, anywhere, anywhere),
        scratch_shapes=scratch,
        compiler_params=pltpu.CompilerParams(
            collective_id=0, has_side_effects=True, vmem_limit_bytes=58 * 1024 * 1024
        ),
        name="experts",
    )(
        expert_hidden,
        jnp.swapaxes(down_weight, 1, 2),
        out_grad,
        expert_ids.T,
        gate_code.T,
        expert_load.reshape(1, LANES),
    )
    mixed, hidden_grad, weight_grad, spare_grad = pl.pallas_call(
        store,
        out_shape=shapes,
        in_specs=[anywhere] * 4,
        out_specs=[anywhere] * 4,
        scratch_shapes=[dma((4,))],
        name="store",
    )(*results)
    return mixed, hidden_grad, jnp.swapaxes(weight_grad, 1, 2), jnp.swapaxes(spare_grad, 1, 2)


def solution(mesh):
    placed = (
        P("expert", None, None),
        P("expert", None, "dp"),
        P("expert", "dp"),
        P("expert", None),
        P("expert", None),
        P(),
    )
    return jax.shard_map(
        body,
        mesh=mesh,
        in_specs=placed,
        out_specs=(
            P("expert", "dp"),
            P("expert", "dp", None),
            P("expert", None, "dp"),
            P("expert", None, "dp"),
        ),
        check_vma=False,
    )
```

```python
import jax
import jax.numpy as jnp
from jax import lax
from jax.experimental import pallas as pl
from jax.experimental.pallas import tpu as pltpu
from jax.sharding import PartitionSpec as P

MESH = pl.DeviceIdType.MESH
BF = jnp.bfloat16
F32 = jnp.float32

Z = 8
X = 8
Y = 8
TOK = 96
LANES = 128
TOP = 8
MOST = 12
H = 1024
COLS = 224
HALF = 384
BLOCK = 48
RING = 7
SIDE = 512


def dot(a, b):
    return jnp.dot(a, b, preferred_element_type=F32)


def dot_nt(a, b):
    return lax.dot_general(a, b, (((1,), (1,)), ((), ())), preferred_element_type=F32)


def dot_tn(a, b):
    return lax.dot_general(a, b, (((0,), (0,)), ((), ())), preferred_element_type=F32)


def kernel(
    hid_hbm, w_hbm, og_ref, ids_ref, code_ref, load_ref,
    mixed_ref, hg_ref, wg_hbm, sg_hbm,
    hid, hid_n, hid_h, hid_c, w, w_n, w_h, w_c,
    meta, tok, perm, perm_h,
    key_n, key_h, key_c, gate_n, gate_h, gate_c, g_n, g_hc, gt_n, gt_hc,
    out_n, out_h, out_c, send_n, send_hc, recv_n, recv_hc,
    sb_n, sb_h, sb_c, back_n, back_hc, rg_n, rg_hc, rgt_n, rgt_hc,
    cxs_n, cxs_h, cxs_c, cxr_n, cxr_h, cxr_c, sum_n, sum_h, sum_c,
    rs_n, rs_h, rs_c, rr_n, rr_h, rr_c,
    mix_s, mix_r, val_h, val_c, wg, sg,
    load_sem, zt_s, zt_r, zm_s, zm_r, wc_s, wc_r,
    dn_s, dn_r, dh_s, dh_r, bn_s, bn_r, bh_s, bh_r, bc_s, bc_r,
    cx_s, cx_r, ring_s, ring_r, mx_s, mx_r, out_sem,
):
    e = lax.axis_index("expert")
    dp = lax.axis_index("dp")
    z, x, y, c = e // X, e % X, dp // 2, dp % 2
    h = z // 4

    def z_peer(d):
        return (((z + d) % Z) * X + x, dp)

    def x_peer(d):
        return (z * X + (x + d) % X, dp)

    def y_peer(d):
        return (e, ((y + d) % Y) * 2 + c)

    sibling = (e, y * 2 + 1 - c)

    def remote(src, dst, s, r, to):
        return pltpu.make_async_remote_copy(
            src_ref=src, dst_ref=dst, send_sem=s, recv_sem=r, device_id=to, device_id_type=MESH
        )

    loads = [
        pltpu.make_async_copy(w_hbm, w, load_sem.at[0]),
        pltpu.make_async_copy(hid_hbm.at[0], hid.at[0], load_sem.at[1]),
        pltpu.make_async_copy(hid_hbm.at[1], hid.at[1], load_sem.at[2]),
        pltpu.make_async_copy(
            hid_hbm.at[2, pl.ds(pl.multiple_of(h * HALF, HALF), HALF)], hid_c, load_sem.at[3]
        ),
    ]
    for copy in loads:
        copy.start()

    barrier = pltpu.get_barrier_semaphore()
    peers = [z_peer(d) for d in range(1, Z)] + [x_peer(d) for d in range(1, X)]
    peers += [y_peer(1), y_peer(-1), sibling]
    for peer in peers:
        pl.semaphore_signal(barrier, inc=1, device_id=peer, device_id_type=MESH)

    meta[z] = jnp.full((2 * TOP, LANES), -1.0, BF)
    facts = jnp.concatenate([ids_ref[...].astype(F32), code_ref[...].astype(F32)], axis=0)
    meta[z, :, 0:TOK] = facts.astype(BF)
    tok[z, 0:TOK] = og_ref[...]
    for i in range(Z):
        tok[i, TOK:LANES] = jnp.zeros((LANES - TOK, COLS), BF)

    pl.semaphore_wait(barrier, len(peers))

    gather = []
    for i, d in enumerate((4, 3, -3, 2, -2, 1, -1)):
        gather.append(remote(meta.at[z], meta.at[z], zm_s.at[i], zm_r.at[i], z_peer(d)))
        gather.append(
            remote(tok.at[z, pl.ds(0, TOK)], tok.at[z, pl.ds(0, TOK)], zt_s.at[i], zt_r.at[i], z_peer(d))
        )
    for copy in gather:
        copy.start()

    lane = lax.broadcasted_iota(jnp.int32, (X, LANES), 1)
    at_x = lax.broadcasted_iota(jnp.int32, (X, 1), 0)
    loads_all = jnp.broadcast_to(load_ref[...].astype(F32), (X, LANES))

    def hottest(row_of_z):
        first = 2 * (row_of_z * X + at_x)
        even = jnp.sum(jnp.where(lane == first, loads_all, 0.0), axis=1, keepdims=True)
        odd = jnp.sum(jnp.where(lane == first + 1, loads_all, 0.0), axis=1, keepdims=True)
        return jnp.where(odd > even, 1.0, 0.0)

    hot_here = hottest(z)
    hot = jnp.sum(jnp.where(at_x == x, hot_here, 0.0), axis=0, keepdims=True)
    hot_b, cold_b = hot.astype(BF), (1.0 - hot).astype(BF)
    cold = 1.0 - hot

    loads[0].wait()
    w_h[...] = w[0] * cold_b + w[1] * hot_b
    w_n[...] = w[0] * hot_b + w[1] * cold_b

    row = lax.broadcasted_iota(jnp.int32, (TOK, 1), 0)
    outer = jnp.zeros((TOK, 1), jnp.int32)
    for k in range(1, 8):
        outer = outer + jnp.where(row >= k * MOST, 1, 0)
    moved = outer * TOK + row - outer * MOST
    col = lax.broadcasted_iota(jnp.int32, (TOK, 2 * HALF), 1)
    for k in range(8):
        perm[k * TOK : (k + 1) * TOK] = jnp.where(col == moved + k * MOST, 1.0, 0.0).astype(BF)
    for k in range(8):
        perm_h[k * BLOCK : (k + 1) * BLOCK] = perm[k * TOK : k * TOK + BLOCK, 0:HALF]

    loads[1].wait()
    loads[2].wait()

    def forward_n(i, carry):
        at = pl.ds(pl.multiple_of(i * 256, 256), 256)
        rows = hid[0, at] * hot_b + hid[1, at] * cold_b
        hid_n[at] = rows
        out_n[at] = dot_nt(rows, w_n[...]).astype(BF)
        return carry

    lax.fori_loop(0, 3, forward_n, 0)
    back = []
    for i in range(2):
        part = dot(perm[i * HALF : (i + 1) * HALF], out_n[...]).astype(BF)
        sb_n[4 * i : 4 * i + 4] = part.reshape(4, TOK, COLS)
    for i, d in enumerate((4, 3, -3, 2, -2, 1, -1)):
        copy = remote(sb_n.at[(x + d) % X], back_n.at[(-d) % X], bn_s.at[i], bn_r.at[i], x_peer(d))
        copy.start()
        back.append(copy)
    back_n[0] = sb_n[x]

    for copy in gather:
        copy.wait()
    spare = remote(w_h, w_c, wc_s.at[0], wc_r.at[0], z_peer(4))
    spare.start()

    far_z = (z + 4) % Z
    home = (2 * (z * X + at_x)).astype(F32)
    name_n = home + 1.0 - hot_here
    name_h = home + hot_here
    name_c = (2 * (far_z * X + at_x)).astype(F32) + hottest(far_z)
    before = jnp.where(
        lax.broadcasted_iota(jnp.int32, (LANES, LANES), 0) < lax.broadcasted_iota(jnp.int32, (LANES, LANES), 1), 1.0, 0.0
    ).astype(BF)

    def match(facts, name):
        hits = jnp.zeros((X, LANES), F32)
        gates = jnp.zeros((X, LANES), F32)
        for k in range(TOP):
            same = facts[k : k + 1, :] == name
            hits = hits + jnp.where(same, 1.0, 0.0)
            gates = gates + jnp.where(same, 0.0625 * (facts[TOP + k : TOP + k + 1, :] + 1.0), 0.0)
        return hits, gates

    def keys(hits, first):
        places = dot(hits.astype(BF), before)
        return jnp.where(hits > 0.5, places + first, -1.0)

    for i in range(Z):
        hits, gates = match(meta[i].astype(F32), name_n)
        key_n[:, i * LANES : (i + 1) * LANES] = keys(hits, float(i * MOST))
        gate_n[:, i * LANES : (i + 1) * LANES] = gates
    for i in range(4):
        facts = meta[4 * h + i].astype(F32)
        hits, gates = match(facts, name_h)
        key_h[:, i * LANES : (i + 1) * LANES] = keys(hits, float(i * MOST))
        gate_h[:, i * LANES : (i + 1) * LANES] = gates
        hits, gates = match(facts, name_c)
        key_c[:, i * LANES : (i + 1) * LANES] = keys(hits, float(BLOCK + i * MOST))
        gate_c[:, i * LANES : (i + 1) * LANES] = gates

    order = (0, 4, 3, 5, 2, 6, 1, 7)
    places_n = lax.broadcasted_iota(jnp.int32, (TOK, Z * LANES), 0).astype(F32)
    dispatch_n = []
    for group in (order[0:4], order[4:8]):
        for d in group:
            at = pl.ds((x + d) % X, 1)
            i = order.index(d)
            g_n[i * TOK : (i + 1) * TOK] = jnp.where(key_n[at, :] == places_n, gate_n[at, :], 0.0).astype(BF)
        i = order.index(group[0])
        rows = dot(g_n[i * TOK : (i + 4) * TOK], tok[...].reshape(Z * LANES, COLS)).astype(BF)
        send_n[i : i + 4] = rows.reshape(4, TOK, COLS)
        for d in group:
            i = order.index(d)
            if d:
                copy = remote(send_n.at[i], recv_n.at[x], dn_s.at[i - 1], dn_r.at[i - 1], x_peer(d))
                copy.start()
                dispatch_n.append(copy)
            else:
                recv_n[x] = send_n[i]
    places_h = lax.broadcasted_iota(jnp.int32, (TOK, 4 * LANES), 0).astype(F32)
    dispatch_h = []
    for group in (order[0:4], order[4:8]):
        for d in group:
            at = pl.ds((x + d) % X, 1)
            i = order.index(d)
            g_hc[i * TOK : (i + 1) * TOK] = (
                jnp.where(key_h[at, :] == places_h, gate_h[at, :], 0.0)
                + jnp.where(key_c[at, :] == places_h, gate_c[at, :], 0.0)
            ).astype(BF)
        i = order.index(group[0])
        rows = dot(g_hc[i * TOK : (i + 4) * TOK], tok[pl.ds(4 * h, 4)].reshape(4 * LANES, COLS)).astype(BF)
        send_hc[i : i + 4] = rows.reshape(4, TOK, COLS)
        for d in group:
            i = order.index(d)
            if d:
                copy = remote(send_hc.at[i], recv_hc.at[x], dh_s.at[i - 1], dh_r.at[i - 1], x_peer(d))
                copy.start()
                dispatch_h.append(copy)
            else:
                recv_hc[x] = send_hc[i]

    def forward_h(i, carry):
        at = pl.ds(pl.multiple_of(i * 128, 128), 128)
        far = pl.ds(pl.multiple_of(h * HALF + i * 128, 128), 128)
        rows = hid[0, far] * cold_b + hid[1, far] * hot_b
        hid_h[at] = rows
        out_h[at] = dot_nt(rows, w_h[...]).astype(BF)
        return carry

    lax.fori_loop(0, 3, forward_h, 0)

    part = dot(perm_h[...], out_h[...]).astype(BF)
    sb_h[...] = part.reshape(X, BLOCK, COLS)
    for i in range(4):
        at = slice(i * 2 * LANES, (i + 1) * 2 * LANES)
        gt_n[at] = g_n[:, at].T
    for i in range(2):
        at = slice(i * 2 * LANES, (i + 1) * 2 * LANES)
        gt_hc[at] = g_hc[:, at].T

    def partial(rg, first, count, weight, cxs, cxr, sums, sem):
        def rows_of(core):
            return jnp.concatenate(
                [
                    rg[pl.ds(pl.multiple_of(first + (2 * t + core) * BLOCK, 16), BLOCK), :]
                    for t in range(count)
                ],
                axis=0,
            )

        theirs = rows_of(1 - c)
        copies = []
        for side in range(2):
            part = dot(theirs, weight[:, side * SIDE : (side + 1) * SIDE]).astype(BF)
            cxs[side] = part.reshape(count, BLOCK, SIDE)
            copy = remote(cxs.at[side], cxr.at[side], cx_s.at[sem + side], cx_r.at[sem + side], sibling)
            copy.start()
            copies.append(copy)
        mine = rows_of(c)
        for side in range(2):
            part = dot(mine, weight[:, side * SIDE : (side + 1) * SIDE])
            sums[side] = part.reshape(count, BLOCK, SIDE)
        return copies

    for copy in dispatch_n:
        copy.wait()
    for i in range(2):
        rows = dot(perm[i * HALF : (i + 1) * HALF], recv_n[...].reshape(2 * HALF, COLS)).astype(BF)
        rg_n[i * HALF : (i + 1) * HALF] = rows
    pair_n = partial(rg_n, 0, 8, w_n, cxs_n, cxr_n, sum_n, 0)

    def at_step(side, k):
        return (y - (1 - 2 * side) * (1 + k)) % Y

    def ring_copy(kind, side, k):
        rs, rr = ((rs_n, rr_n), (rs_h, rr_h), (rs_c, rr_c))[kind]
        i = (kind * 2 + side) * RING + k
        return remote(rs.at[side, k], rr.at[side, k], ring_s.at[i], ring_r.at[i], y_peer(1 - 2 * side))

    def block_sum(kind, side, t, k):
        sums, cxr, rr = ((sum_n, cxr_n, rr_n), (sum_h, cxr_h, rr_h), (sum_c, cxr_c, rr_c))[kind]
        total = sums[side, t] + cxr[side, t].astype(F32)
        if k > 0:
            total = total + rr[side, k - 1].astype(F32)
        return total

    def ring_step(kind, k):
        rs = (rs_n, rs_h, rs_c)[kind]
        for side in range(2):
            t = at_step(side, k)

            def go(side=side, t=t):
                if k > 0:
                    ring_copy(kind, side, k - 1).wait_recv()
                rs[side, k] = block_sum(kind, side, t if kind == 0 else t % 4, k).astype(BF)
                ring_copy(kind, side, k).start()

            if kind == 0:
                go()
            else:
                pl.when(t // 4 == h)(go)

    def ring_end(kind):
        for side in range(2):
            for k in range(RING):
                if kind == 0:
                    ring_copy(kind, side, k).wait_send()
                else:

                    @pl.when(at_step(side, k) // 4 == h)
                    def _(side=side, k=k):
                        ring_copy(kind, side, k).wait_send()

    for i, d in enumerate((4, 3, -3, 2, -2, 1, -1)):
        copy = remote(
            sb_h.at[(x + d) % X], back_hc.at[order.index((-d) % X), pl.ds(0, BLOCK)], bh_s.at[i], bh_r.at[i], x_peer(d)
        )
        copy.start()
        back.append(copy)
    back_hc[0, 0:BLOCK] = sb_h[x]

    for copy in pair_n:
        copy.wait()
    ring_step(0, 0)
    ring_step(0, 1)

    for copy in dispatch_h:
        copy.wait()
    for i in range(2):
        rows = dot(perm[i * HALF : (i + 1) * HALF], recv_hc[...].reshape(2 * HALF, COLS)).astype(BF)
        rg_hc[i * HALF : (i + 1) * HALF] = rows
    pair_h = partial(rg_hc, 0, 4, w_h, cxs_h, cxr_h, sum_h, 2)
    ring_step(0, 2)
    for copy in pair_h:
        copy.wait()
    ring_step(1, 0)
    ring_step(0, 3)
    ring_step(1, 1)

    spare.wait()
    loads[3].wait()

    def forward_c(i, carry):
        at = pl.ds(pl.multiple_of(i * 128, 128), 128)
        out_c[at] = dot_nt(hid_c[at], w_c[...]).astype(BF)
        return carry

    lax.fori_loop(0, 3, forward_c, 0)
    part = dot(perm_h[...], out_c[...]).astype(BF)
    sb_c[...] = part.reshape(X, BLOCK, COLS)
    for i, d in enumerate((4, 3, -3, 2, -2, 1, -1)):
        copy = remote(
            sb_c.at[(x + d) % X], back_hc.at[order.index((-d) % X), pl.ds(BLOCK, BLOCK)], bc_s.at[i], bc_r.at[i], x_peer(d)
        )
        copy.start()
        back.append(copy)
    back_hc[0, BLOCK:TOK] = sb_c[x]
    pair_c = partial(rg_hc, HALF, 4, w_c, cxs_c, cxr_c, sum_c, 4)
    ring_step(0, 4)
    ring_step(1, 2)
    for copy in pair_c:
        copy.wait()
    ring_step(2, 0)

    scale = 2.0 / TOK

    def turn_rows():
        rgt_n[...] = rg_n[...].T
        rgt_hc[...] = rg_hc[...].T

    def weight_part(i):
        at = slice(i * SIDE, (i + 1) * SIDE)
        grad_n = scale * dot(rgt_n[...], hid_n[:, at])
        grad_h = scale * dot(rgt_hc[:, 0:HALF], hid_h[:, at])
        wg[0, :, at] = (grad_n * hot + grad_h * cold).astype(BF)
        wg[1, :, at] = (grad_n * cold + grad_h * hot).astype(BF)
        sg[0, :, at] = (scale * dot(rgt_hc[:, HALF : 2 * HALF], hid_c[:, at])).astype(BF)

    turn_rows()
    ring_step(0, 5)
    ring_step(1, 3)
    ring_step(2, 1)
    for copy in back[0:7]:
        copy.wait()
    rows = jnp.concatenate([back_n[d] for d in order], axis=0)
    mix_s[...] = dot(gt_n[...], rows).reshape(Z, LANES, COLS)[:, 0:TOK]
    ring_step(0, 6)
    ring_step(1, 4)
    ring_step(2, 2)
    for copy in back[7:]:
        copy.wait()
    near = dot(gt_hc[...], back_hc[...].reshape(X * TOK, COLS)).reshape(4, LANES, COLS)
    mix_s[pl.ds(4 * h, 4)] = mix_s[pl.ds(4 * h, 4)] + near[:, 0:TOK]
    mix = []
    for i, d in enumerate((4, 3, -3, 2, -2, 1, -1)):
        mix_r[8 + i] = mix_s[(z + d) % Z].astype(BF)
        copy = remote(mix_r.at[8 + i], mix_r.at[i], mx_s.at[i], mx_r.at[i], z_peer(d))
        copy.start()
        mix.append(copy)
    ring_step(1, 5)
    ring_step(2, 3)
    weight_part(0)
    ring_step(1, 6)
    ring_step(2, 4)
    weight_part(1)
    stores = [
        pltpu.make_async_copy(wg, wg_hbm, out_sem.at[0]),
        pltpu.make_async_copy(sg, sg_hbm, out_sem.at[1]),
    ]
    for copy in stores:
        copy.start()
    ring_step(2, 5)
    ring_step(2, 6)

    val_h[...] = jnp.zeros_like(val_h)
    val_c[...] = jnp.zeros_like(val_c)
    value_n = []
    for side in range(2):
        ring_copy(0, side, RING - 1).wait_recv()
        value_n.append(block_sum(0, side, y, RING))

    @pl.when(y // 4 == h)
    def _():
        for side in range(2):
            at = slice(side * SIDE, (side + 1) * SIDE)
            ring_copy(1, side, RING - 1).wait_recv()
            val_h[:, at] = block_sum(1, side, y % 4, RING)
            ring_copy(2, side, RING - 1).wait_recv()
            val_c[:, at] = block_sum(2, side, y % 4, RING)

    for side in range(2):
        at = slice(side * SIDE, (side + 1) * SIDE)
        hg_ref[0, :, at] = (value_n[side] * hot + val_h[:, at] * cold).astype(BF)
        hg_ref[1, :, at] = (value_n[side] * cold + val_h[:, at] * hot).astype(BF)
    hg_ref[2] = val_c[...].astype(BF)

    total = mix_s[z]
    for copy in mix:
        copy.wait()
    for i in range(Z - 1):
        total = total + mix_r[i].astype(F32)
    mixed_ref[...] = total.astype(BF)

    for kind in range(3):
        ring_end(kind)
    for copy in stores:
        copy.wait()


def store(*refs):
    given, results, held, sem = refs[0:4], refs[4:8], refs[8:12], refs[12]
    inward = [pltpu.make_async_copy(given[i], held[i], sem.at[i]) for i in range(4)]
    outward = [pltpu.make_async_copy(held[i], results[i], sem.at[4 + i]) for i in range(4)]
    for i in range(4):
        inward[i].start()
    for i in range(4):
        inward[i].wait()
        outward[i].start()
    for i in range(4):
        outward[i].wait()


def body(expert_hidden, down_weight, out_grad, expert_ids, gate_code, expert_load):
    vmem = pl.BlockSpec(memory_space=pltpu.VMEM)
    anywhere = pl.BlockSpec(memory_space=pl.ANY)
    dma = pltpu.SemaphoreType.DMA

    def b(*shape):
        return pltpu.VMEM(shape, BF)

    def f(*shape):
        return pltpu.VMEM(shape, F32)

    scratch = [
        b(2, 2 * HALF, H), b(2 * HALF, H), b(HALF, H), b(HALF, H),
        b(2, COLS, H), b(COLS, H), b(COLS, H), b(COLS, H),
        b(Z, 2 * TOP, LANES), b(Z, LANES, COLS), b(2 * HALF, 2 * HALF), b(HALF, HALF),
        f(X, Z * LANES), f(X, 4 * LANES), f(X, 4 * LANES), f(X, Z * LANES), f(X, 4 * LANES), f(X, 4 * LANES),
        b(X * TOK, Z * LANES), b(X * TOK, 4 * LANES), b(Z * LANES, X * TOK), b(4 * LANES, X * TOK),
        b(2 * HALF, COLS), b(HALF, COLS), b(HALF, COLS),
        b(X, TOK, COLS), b(X, TOK, COLS), b(X, TOK, COLS), b(X, TOK, COLS),
        b(X, TOK, COLS), b(X, BLOCK, COLS), b(X, BLOCK, COLS), b(X, TOK, COLS), b(X, TOK, COLS),
        b(2 * HALF, COLS), b(2 * HALF, COLS), b(COLS, 2 * HALF), b(COLS, 2 * HALF),
        b(2, 8, BLOCK, SIDE), b(2, 4, BLOCK, SIDE), b(2, 4, BLOCK, SIDE),
        b(2, 8, BLOCK, SIDE), b(2, 4, BLOCK, SIDE), b(2, 4, BLOCK, SIDE),
        f(2, 8, BLOCK, SIDE), f(2, 4, BLOCK, SIDE), f(2, 4, BLOCK, SIDE),
        b(2, RING, BLOCK, SIDE), b(2, RING, BLOCK, SIDE), b(2, RING, BLOCK, SIDE),
        b(2, RING, BLOCK, SIDE), b(2, RING, BLOCK, SIDE), b(2, RING, BLOCK, SIDE),
        f(Z, TOK, COLS), b(2 * Z, TOK, COLS), f(BLOCK, H), f(BLOCK, H), b(2, COLS, H), b(1, COLS, H),
        dma((4,)), dma((7,)), dma((7,)), dma((7,)), dma((7,)), dma((1,)), dma((1,)),
        dma((7,)), dma((7,)), dma((7,)), dma((7,)), dma((7,)), dma((7,)), dma((7,)), dma((7,)), dma((7,)), dma((7,)),
        dma((6,)), dma((6,)), dma((6 * RING,)), dma((6 * RING,)), dma((7,)), dma((7,)), dma((2,)),
    ]
    shapes = (
        jax.ShapeDtypeStruct((TOK, COLS), BF),
        jax.ShapeDtypeStruct((3, BLOCK, H), BF),
        jax.ShapeDtypeStruct((2, COLS, H), BF),
        jax.ShapeDtypeStruct((1, COLS, H), BF),
    )
    results = pl.pallas_call(
        kernel,
        out_shape=shapes,
        in_specs=[anywhere, anywhere, vmem, vmem, vmem, vmem],
        out_specs=(vmem, vmem, anywhere, anywhere),
        scratch_shapes=scratch,
        compiler_params=pltpu.CompilerParams(
            collective_id=0, has_side_effects=True, vmem_limit_bytes=58 * 1024 * 1024
        ),
        name="experts",
    )(
        expert_hidden,
        jnp.swapaxes(down_weight, 1, 2),
        out_grad,
        expert_ids.T,
        gate_code.T,
        expert_load.reshape(1, LANES),
    )
    mixed, hidden_grad, weight_grad, spare_grad = pl.pallas_call(
        store,
        out_shape=shapes,
        in_specs=[anywhere] * 4,
        out_specs=[anywhere] * 4,
        scratch_shapes=[b(TOK, COLS), b(3, BLOCK, H), b(2, COLS, H), b(1, COLS, H), dma((8,))],
        name="store",
    )(*results)
    return mixed, hidden_grad, jnp.swapaxes(weight_grad, 1, 2), jnp.swapaxes(spare_grad, 1, 2)


def solution(mesh):
    placed = (
        P("expert", None, None),
        P("expert", None, "dp"),
        P("expert", "dp"),
        P("expert", None),
        P("expert", None),
        P(),
    )
    return jax.shard_map(
        body,
        mesh=mesh,
        in_specs=placed,
        out_specs=(
            P("expert", "dp"),
            P("expert", "dp", None),
            P("expert", None, "dp"),
            P("expert", None, "dp"),
        ),
        check_vma=False,
    )
```

```python
import jax
import jax.numpy as jnp
from jax import lax
from jax.experimental import pallas as pl
from jax.experimental.pallas import tpu as pltpu
from jax.sharding import PartitionSpec as P

MESH = pl.DeviceIdType.MESH
BF = jnp.bfloat16
F32 = jnp.float32

Z = 8
X = 8
Y = 8
TOK = 96
LANES = 128
TOP = 8
MOST = 12
H = 1024
COLS = 224
HALF = 384
BLOCK = 48
RING = 7
SIDE = 512


def dot(a, b):
    return jnp.dot(a, b, preferred_element_type=F32)


def dot_nt(a, b):
    return lax.dot_general(a, b, (((1,), (1,)), ((), ())), preferred_element_type=F32)


def dot_tn(a, b):
    return lax.dot_general(a, b, (((0,), (0,)), ((), ())), preferred_element_type=F32)


def kernel(
    hid_hbm, w_hbm, og_ref, ids_ref, code_ref, load_ref,
    mixed_ref, hg_ref, wg_hbm, sg_hbm,
    hid, hid_n, hid_h, hid_c, w, w_n, w_h, w_c,
    meta, tok, perm, perm_h,
    key_n, key_h, key_c, gate_n, gate_h, gate_c, g_n, g_hc, gt_n, gt_h, gt_c,
    out_n, out_h, out_c, send_n, send_hc, recv_n, recv_hc,
    sb_n, sb_h, sb_c, back_n, back_h, back_c, rg_n, rg_hc, rgt_n, rgt_hc,
    cxs_n, cxs_h, cxs_c, cxr_n, cxr_h, cxr_c, sum_n, sum_h, sum_c,
    rs_n, rs_h, rs_c, rr_n, rr_h, rr_c,
    mix_s, mix_r, mix_c, mixc_r, val_h, val_c, wg, sg,
    load_sem, zt_s, zt_r, zm_s, zm_r, wc_s, wc_r,
    dn_s, dn_r, dh_s, dh_r, bn_s, bn_r, bh_s, bh_r, bc_s, bc_r,
    cx_s, cx_r, ring_s, ring_r, mx_s, mx_r, mxc_s, mxc_r, out_sem,
):
    e = lax.axis_index("expert")
    dp = lax.axis_index("dp")
    z, x, y, c = e // X, e % X, dp // 2, dp % 2
    h = z // 4

    def z_peer(d):
        return (((z + d) % Z) * X + x, dp)

    def x_peer(d):
        return (z * X + (x + d) % X, dp)

    def y_peer(d):
        return (e, ((y + d) % Y) * 2 + c)

    sibling = (e, y * 2 + 1 - c)

    def remote(src, dst, s, r, to):
        return pltpu.make_async_remote_copy(
            src_ref=src, dst_ref=dst, send_sem=s, recv_sem=r, device_id=to, device_id_type=MESH
        )

    loads = [
        pltpu.make_async_copy(w_hbm, w, load_sem.at[0]),
        pltpu.make_async_copy(hid_hbm.at[0], hid.at[0], load_sem.at[1]),
        pltpu.make_async_copy(hid_hbm.at[1], hid.at[1], load_sem.at[2]),
        pltpu.make_async_copy(
            hid_hbm.at[2, pl.ds(pl.multiple_of(h * HALF, HALF), HALF)], hid_c, load_sem.at[3]
        ),
    ]
    for copy in loads:
        copy.start()

    barrier = pltpu.get_barrier_semaphore()
    peers = [z_peer(d) for d in range(1, Z)] + [x_peer(d) for d in range(1, X)]
    peers += [y_peer(1), y_peer(-1), sibling]
    for peer in peers:
        pl.semaphore_signal(barrier, inc=1, device_id=peer, device_id_type=MESH)

    meta[z] = jnp.full((2 * TOP, LANES), -1.0, BF)
    facts = jnp.concatenate([ids_ref[...].astype(F32), code_ref[...].astype(F32)], axis=0)
    meta[z, :, 0:TOK] = facts.astype(BF)
    tok[z, 0:TOK] = og_ref[...]
    for i in range(Z):
        tok[i, TOK:LANES] = jnp.zeros((LANES - TOK, COLS), BF)

    pl.semaphore_wait(barrier, len(peers))

    near = [4 * h + (z + i) % 4 for i in range(1, 4)]
    far = [4 * (1 - h) + (z + i) % 4 for i in range(4)]
    gather = []
    for i, other in enumerate(near + far):
        peer = (other * X + x, dp)
        gather.append(remote(meta.at[z], meta.at[z], zm_s.at[i], zm_r.at[i], peer))
        gather.append(
            remote(tok.at[z, pl.ds(0, TOK)], tok.at[z, pl.ds(0, TOK)], zt_s.at[i], zt_r.at[i], peer)
        )
    for copy in gather:
        copy.start()

    lane = lax.broadcasted_iota(jnp.int32, (X, LANES), 1)
    at_x = lax.broadcasted_iota(jnp.int32, (X, 1), 0)
    loads_all = jnp.broadcast_to(load_ref[...].astype(F32), (X, LANES))

    def hottest(row_of_z):
        first = 2 * (row_of_z * X + at_x)
        even = jnp.sum(jnp.where(lane == first, loads_all, 0.0), axis=1, keepdims=True)
        odd = jnp.sum(jnp.where(lane == first + 1, loads_all, 0.0), axis=1, keepdims=True)
        return jnp.where(odd > even, 1.0, 0.0)

    hot_here = hottest(z)
    hot = jnp.sum(jnp.where(at_x == x, hot_here, 0.0), axis=0, keepdims=True)
    hot_b, cold_b = hot.astype(BF), (1.0 - hot).astype(BF)
    cold = 1.0 - hot

    loads[0].wait()
    w_h[...] = w[0] * cold_b + w[1] * hot_b
    w_n[...] = w[0] * hot_b + w[1] * cold_b

    row = lax.broadcasted_iota(jnp.int32, (TOK, 1), 0)
    outer = jnp.zeros((TOK, 1), jnp.int32)
    for k in range(1, 8):
        outer = outer + jnp.where(row >= k * MOST, 1, 0)
    moved = outer * TOK + row - outer * MOST
    col = lax.broadcasted_iota(jnp.int32, (TOK, 2 * HALF), 1)
    for k in range(8):
        perm[k * TOK : (k + 1) * TOK] = jnp.where(col == moved + k * MOST, 1.0, 0.0).astype(BF)
    for k in range(8):
        perm_h[k * BLOCK : (k + 1) * BLOCK] = perm[k * TOK : k * TOK + BLOCK, 0:HALF]

    loads[1].wait()
    loads[2].wait()

    def forward_n(i, carry):
        at = pl.ds(pl.multiple_of(i * 256, 256), 256)
        rows = hid[0, at] * hot_b + hid[1, at] * cold_b
        hid_n[at] = rows
        out_n[at] = dot_nt(rows, w_n[...]).astype(BF)
        return carry

    lax.fori_loop(0, 3, forward_n, 0)
    back = []
    for i in range(2):
        part = dot(perm[i * HALF : (i + 1) * HALF], out_n[...]).astype(BF)
        sb_n[4 * i : 4 * i + 4] = part.reshape(4, TOK, COLS)
    for i, d in enumerate((4, 3, -3, 2, -2, 1, -1)):
        copy = remote(sb_n.at[(x + d) % X], back_n.at[(-d) % X], bn_s.at[i], bn_r.at[i], x_peer(d))
        copy.start()
        back.append(copy)
    back_n[0] = sb_n[x]

    for copy in gather[0:6]:
        copy.wait()
    spare = remote(w_h, w_c, wc_s.at[0], wc_r.at[0], z_peer(4))
    spare.start()

    far_z = (z + 4) % Z
    home = (2 * (z * X + at_x)).astype(F32)
    name_n = home + 1.0 - hot_here
    name_h = home + hot_here
    name_c = (2 * (far_z * X + at_x)).astype(F32) + hottest(far_z)
    before = jnp.where(
        lax.broadcasted_iota(jnp.int32, (LANES, LANES), 0) < lax.broadcasted_iota(jnp.int32, (LANES, LANES), 1), 1.0, 0.0
    ).astype(BF)

    def match(facts, name):
        hits = jnp.zeros((X, LANES), F32)
        gates = jnp.zeros((X, LANES), F32)
        for k in range(TOP):
            same = facts[k : k + 1, :] == name
            hits = hits + jnp.where(same, 1.0, 0.0)
            gates = gates + jnp.where(same, 0.0625 * (facts[TOP + k : TOP + k + 1, :] + 1.0), 0.0)
        return hits, gates

    def keys(hits, first):
        places = dot(hits.astype(BF), before)
        return jnp.where(hits > 0.5, places + first, -1.0)

    for i in range(4):
        facts = meta[4 * h + i].astype(F32)
        hits, gates = match(facts, name_h)
        key_h[:, i * LANES : (i + 1) * LANES] = keys(hits, float(i * MOST))
        gate_h[:, i * LANES : (i + 1) * LANES] = gates
        hits, gates = match(facts, name_c)
        key_c[:, i * LANES : (i + 1) * LANES] = keys(hits, float(BLOCK + i * MOST))
        gate_c[:, i * LANES : (i + 1) * LANES] = gates

    order = (0, 4, 3, 5, 2, 6, 1, 7)
    places_h = lax.broadcasted_iota(jnp.int32, (TOK, 4 * LANES), 0).astype(F32)
    dispatch_h = []
    for group in (order[0:4], order[4:8]):
        for d in group:
            at = pl.ds((x + d) % X, 1)
            i = order.index(d)
            g_hc[i * TOK : (i + 1) * TOK] = (
                jnp.where(key_h[at, :] == places_h, gate_h[at, :], 0.0)
                + jnp.where(key_c[at, :] == places_h, gate_c[at, :], 0.0)
            ).astype(BF)
        i = order.index(group[0])
        rows = dot(g_hc[i * TOK : (i + 4) * TOK], tok[pl.ds(4 * h, 4)].reshape(4 * LANES, COLS)).astype(BF)
        send_hc[i : i + 4] = rows.reshape(4, TOK, COLS)
        for d in group:
            i = order.index(d)
            if d:
                copy = remote(send_hc.at[i], recv_hc.at[x], dh_s.at[i - 1], dh_r.at[i - 1], x_peer(d))
                copy.start()
                dispatch_h.append(copy)
            else:
                recv_hc[x] = send_hc[i]

    for copy in gather[6:]:
        copy.wait()
    for i in range(Z):
        hits, gates = match(meta[i].astype(F32), name_n)
        key_n[:, i * LANES : (i + 1) * LANES] = keys(hits, float(i * MOST))
        gate_n[:, i * LANES : (i + 1) * LANES] = gates
    places_n = lax.broadcasted_iota(jnp.int32, (TOK, Z * LANES), 0).astype(F32)
    dispatch_n = []
    for group in (order[0:4], order[4:8]):
        for d in group:
            at = pl.ds((x + d) % X, 1)
            i = order.index(d)
            g_n[i * TOK : (i + 1) * TOK] = jnp.where(key_n[at, :] == places_n, gate_n[at, :], 0.0).astype(BF)
        i = order.index(group[0])
        rows = dot(g_n[i * TOK : (i + 4) * TOK], tok[...].reshape(Z * LANES, COLS)).astype(BF)
        send_n[i : i + 4] = rows.reshape(4, TOK, COLS)
        for d in group:
            i = order.index(d)
            if d:
                copy = remote(send_n.at[i], recv_n.at[x], dn_s.at[i - 1], dn_r.at[i - 1], x_peer(d))
                copy.start()
                dispatch_n.append(copy)
            else:
                recv_n[x] = send_n[i]

    def forward_h(i, carry):
        at = pl.ds(pl.multiple_of(i * 128, 128), 128)
        far = pl.ds(pl.multiple_of(h * HALF + i * 128, 128), 128)
        rows = hid[0, far] * cold_b + hid[1, far] * hot_b
        hid_h[at] = rows
        out_h[at] = dot_nt(rows, w_h[...]).astype(BF)
        return carry

    lax.fori_loop(0, 3, forward_h, 0)

    part = dot(perm_h[...], out_h[...]).astype(BF)
    sb_h[...] = part.reshape(X, BLOCK, COLS)
    for i in range(4):
        at = slice(i * 2 * LANES, (i + 1) * 2 * LANES)
        gt_n[at] = g_n[:, at].T
    for i in range(2):
        at = slice(i * 2 * LANES, (i + 1) * 2 * LANES)
        both = g_hc[:, at].reshape(X, TOK, 2 * LANES)
        gt_h[at] = both[:, 0:BLOCK].reshape(HALF, 2 * LANES).T
        gt_c[at] = both[:, BLOCK:TOK].reshape(HALF, 2 * LANES).T

    def partial(rg, first, count, weight, cxs, cxr, sums, sem):
        def rows_of(core):
            return jnp.concatenate(
                [
                    rg[pl.ds(pl.multiple_of(first + (2 * t + core) * BLOCK, 16), BLOCK), :]
                    for t in range(count)
                ],
                axis=0,
            )

        theirs = rows_of(1 - c)
        copies = []
        for side in range(2):
            part = dot(theirs, weight[:, side * SIDE : (side + 1) * SIDE]).astype(BF)
            cxs[side] = part.reshape(count, BLOCK, SIDE)
            copy = remote(cxs.at[side], cxr.at[side], cx_s.at[sem + side], cx_r.at[sem + side], sibling)
            copy.start()
            copies.append(copy)
        mine = rows_of(c)
        for side in range(2):
            part = dot(mine, weight[:, side * SIDE : (side + 1) * SIDE])
            sums[side] = part.reshape(count, BLOCK, SIDE)
        return copies

    def at_step(side, k):
        return (y - (1 - 2 * side) * (1 + k)) % Y

    def ring_copy(kind, side, k):
        rs, rr = ((rs_n, rr_n), (rs_h, rr_h), (rs_c, rr_c))[kind]
        i = (kind * 2 + side) * RING + k
        return remote(rs.at[side, k], rr.at[side, k], ring_s.at[i], ring_r.at[i], y_peer(1 - 2 * side))

    def block_sum(kind, side, t, k):
        sums, cxr, rr = ((sum_n, cxr_n, rr_n), (sum_h, cxr_h, rr_h), (sum_c, cxr_c, rr_c))[kind]
        total = sums[side, t] + cxr[side, t].astype(F32)
        if k > 0:
            total = total + rr[side, k - 1].astype(F32)
        return total

    def ring_step(kind, k):
        rs = (rs_n, rs_h, rs_c)[kind]
        for side in range(2):
            t = at_step(side, k)

            def go(side=side, t=t):
                if k > 0:
                    ring_copy(kind, side, k - 1).wait_recv()
                rs[side, k] = block_sum(kind, side, t if kind == 0 else t % 4, k).astype(BF)
                ring_copy(kind, side, k).start()

            if kind == 0:
                go()
            else:
                pl.when(t // 4 == h)(go)

    def ring_end(kind):
        for side in range(2):
            for k in range(RING):
                if kind == 0:
                    ring_copy(kind, side, k).wait_send()
                else:

                    @pl.when(at_step(side, k) // 4 == h)
                    def _(side=side, k=k):
                        ring_copy(kind, side, k).wait_send()

    for copy in dispatch_h:
        copy.wait()
    for i in range(2):
        rows = dot(perm[i * HALF : (i + 1) * HALF], recv_hc[...].reshape(2 * HALF, COLS)).astype(BF)
        rg_hc[i * HALF : (i + 1) * HALF] = rows
    pair_h = partial(rg_hc, 0, 4, w_h, cxs_h, cxr_h, sum_h, 2)
    for i, d in enumerate((4, 3, -3, 2, -2, 1, -1)):
        copy = remote(
            sb_h.at[(x + d) % X], back_h.at[order.index((-d) % X)], bh_s.at[i], bh_r.at[i], x_peer(d)
        )
        copy.start()
        back.append(copy)
    back_h[0] = sb_h[x]
    for copy in pair_h:
        copy.wait()
    ring_step(1, 0)
    ring_step(1, 1)
    for copy in dispatch_n:
        copy.wait()
    for i in range(2):
        rows = dot(perm[i * HALF : (i + 1) * HALF], recv_n[...].reshape(2 * HALF, COLS)).astype(BF)
        rg_n[i * HALF : (i + 1) * HALF] = rows
    pair_n = partial(rg_n, 0, 8, w_n, cxs_n, cxr_n, sum_n, 0)
    ring_step(1, 2)
    for copy in pair_n:
        copy.wait()
    ring_step(0, 0)

    spare.wait()
    loads[3].wait()

    def forward_c(i, carry):
        at = pl.ds(pl.multiple_of(i * 128, 128), 128)
        out_c[at] = dot_nt(hid_c[at], w_c[...]).astype(BF)
        return carry

    lax.fori_loop(0, 3, forward_c, 0)
    part = dot(perm_h[...], out_c[...]).astype(BF)
    sb_c[...] = part.reshape(X, BLOCK, COLS)
    for i, d in enumerate((4, 3, -3, 2, -2, 1, -1)):
        copy = remote(
            sb_c.at[(x + d) % X], back_c.at[order.index((-d) % X)], bc_s.at[i], bc_r.at[i], x_peer(d)
        )
        copy.start()
        back.append(copy)
    back_c[0] = sb_c[x]
    pair_c = partial(rg_hc, HALF, 4, w_c, cxs_c, cxr_c, sum_c, 4)
    ring_step(1, 3)
    ring_step(0, 1)
    for copy in pair_c:
        copy.wait()
    ring_step(2, 0)

    scale = 2.0 / TOK

    def turn_rows():
        rgt_n[...] = rg_n[...].T
        rgt_hc[...] = rg_hc[...].T

    def weight_part(i):
        at = slice(i * SIDE, (i + 1) * SIDE)
        grad_n = scale * dot(rgt_n[...], hid_n[:, at])
        grad_h = scale * dot(rgt_hc[:, 0:HALF], hid_h[:, at])
        wg[0, :, at] = (grad_n * hot + grad_h * cold).astype(BF)
        wg[1, :, at] = (grad_n * cold + grad_h * hot).astype(BF)
        sg[0, :, at] = (scale * dot(rgt_hc[:, HALF : 2 * HALF], hid_c[:, at])).astype(BF)

    turn_rows()
    ring_step(1, 4)
    ring_step(0, 2)
    ring_step(2, 1)
    weight_part(0)
    ring_step(1, 5)
    ring_step(0, 3)
    ring_step(2, 2)
    weight_part(1)
    stores = [
        pltpu.make_async_copy(wg, wg_hbm, out_sem.at[0]),
        pltpu.make_async_copy(sg, sg_hbm, out_sem.at[1]),
    ]
    for copy in stores:
        copy.start()
    ring_step(1, 6)
    ring_step(0, 4)
    ring_step(2, 3)

    for copy in back[0:14]:
        copy.wait()
    rows = jnp.concatenate([back_n[d] for d in order], axis=0)
    mix_s[...] = dot(gt_n[...], rows).reshape(Z, LANES, COLS)[:, 0:TOK]
    added = dot(gt_h[...], back_h[...].reshape(HALF, COLS)).reshape(4, LANES, COLS)
    mix_s[pl.ds(4 * h, 4)] = mix_s[pl.ds(4 * h, 4)] + added[:, 0:TOK]
    mix = []
    for i, other in enumerate(near + far):
        mix_r[8 + i] = mix_s[other].astype(BF)
        copy = remote(mix_r.at[8 + i], mix_r.at[i], mx_s.at[i], mx_r.at[i], (other * X + x, dp))
        copy.start()
        mix.append(copy)
    ring_step(0, 5)
    ring_step(2, 4)
    for copy in back[14:]:
        copy.wait()
    mix_c[...] = dot(gt_c[...], back_c[...].reshape(HALF, COLS)).reshape(4, LANES, COLS)[:, 0:TOK]
    for i, other in enumerate(near):
        mixc_r[4 + i] = mix_c[other % 4].astype(BF)
        copy = remote(mixc_r.at[4 + i], mixc_r.at[i], mxc_s.at[i], mxc_r.at[i], (other * X + x, dp))
        copy.start()
        mix.append(copy)
    ring_step(0, 6)
    ring_step(2, 5)
    ring_step(2, 6)

    val_h[...] = jnp.zeros_like(val_h)
    val_c[...] = jnp.zeros_like(val_c)
    value_n = []
    for side in range(2):
        ring_copy(0, side, RING - 1).wait_recv()
        value_n.append(block_sum(0, side, y, RING))

    @pl.when(y // 4 == h)
    def _():
        for side in range(2):
            at = slice(side * SIDE, (side + 1) * SIDE)
            ring_copy(1, side, RING - 1).wait_recv()
            val_h[:, at] = block_sum(1, side, y % 4, RING)
            ring_copy(2, side, RING - 1).wait_recv()
            val_c[:, at] = block_sum(2, side, y % 4, RING)

    for side in range(2):
        at = slice(side * SIDE, (side + 1) * SIDE)
        hg_ref[0, :, at] = (value_n[side] * hot + val_h[:, at] * cold).astype(BF)
        hg_ref[1, :, at] = (value_n[side] * cold + val_h[:, at] * hot).astype(BF)
    hg_ref[2] = val_c[...].astype(BF)

    total = mix_s[z] + mix_c[z % 4]
    for copy in mix:
        copy.wait()
    for i in range(Z - 1):
        total = total + mix_r[i].astype(F32)
    for i in range(3):
        total = total + mixc_r[i].astype(F32)
    mixed_ref[...] = total.astype(BF)

    for kind in range(3):
        ring_end(kind)
    for copy in stores:
        copy.wait()


def store(*refs):
    given, results, held, sem = refs[0:4], refs[4:8], refs[8:12], refs[12]
    inward = [pltpu.make_async_copy(given[i], held[i], sem.at[i]) for i in range(4)]
    outward = [pltpu.make_async_copy(held[i], results[i], sem.at[4 + i]) for i in range(4)]
    for i in range(4):
        inward[i].start()
    for i in range(4):
        inward[i].wait()
        outward[i].start()
    for i in range(4):
        outward[i].wait()


def body(expert_hidden, down_weight, out_grad, expert_ids, gate_code, expert_load):
    vmem = pl.BlockSpec(memory_space=pltpu.VMEM)
    anywhere = pl.BlockSpec(memory_space=pl.ANY)
    dma = pltpu.SemaphoreType.DMA

    def b(*shape):
        return pltpu.VMEM(shape, BF)

    def f(*shape):
        return pltpu.VMEM(shape, F32)

    scratch = [
        b(2, 2 * HALF, H), b(2 * HALF, H), b(HALF, H), b(HALF, H),
        b(2, COLS, H), b(COLS, H), b(COLS, H), b(COLS, H),
        b(Z, 2 * TOP, LANES), b(Z, LANES, COLS), b(2 * HALF, 2 * HALF), b(HALF, HALF),
        f(X, Z * LANES), f(X, 4 * LANES), f(X, 4 * LANES), f(X, Z * LANES), f(X, 4 * LANES), f(X, 4 * LANES),
        b(X * TOK, Z * LANES), b(X * TOK, 4 * LANES), b(Z * LANES, X * TOK), b(4 * LANES, HALF), b(4 * LANES, HALF),
        b(2 * HALF, COLS), b(HALF, COLS), b(HALF, COLS),
        b(X, TOK, COLS), b(X, TOK, COLS), b(X, TOK, COLS), b(X, TOK, COLS),
        b(X, TOK, COLS), b(X, BLOCK, COLS), b(X, BLOCK, COLS), b(X, TOK, COLS), b(X, BLOCK, COLS), b(X, BLOCK, COLS),
        b(2 * HALF, COLS), b(2 * HALF, COLS), b(COLS, 2 * HALF), b(COLS, 2 * HALF),
        b(2, 8, BLOCK, SIDE), b(2, 4, BLOCK, SIDE), b(2, 4, BLOCK, SIDE),
        b(2, 8, BLOCK, SIDE), b(2, 4, BLOCK, SIDE), b(2, 4, BLOCK, SIDE),
        f(2, 8, BLOCK, SIDE), f(2, 4, BLOCK, SIDE), f(2, 4, BLOCK, SIDE),
        b(2, RING, BLOCK, SIDE), b(2, RING, BLOCK, SIDE), b(2, RING, BLOCK, SIDE),
        b(2, RING, BLOCK, SIDE), b(2, RING, BLOCK, SIDE), b(2, RING, BLOCK, SIDE),
        f(Z, TOK, COLS), b(2 * Z, TOK, COLS), f(4, TOK, COLS), b(8, TOK, COLS), f(BLOCK, H), f(BLOCK, H), b(2, COLS, H), b(1, COLS, H),
        dma((4,)), dma((7,)), dma((7,)), dma((7,)), dma((7,)), dma((1,)), dma((1,)),
        dma((7,)), dma((7,)), dma((7,)), dma((7,)), dma((7,)), dma((7,)), dma((7,)), dma((7,)), dma((7,)), dma((7,)),
        dma((6,)), dma((6,)), dma((6 * RING,)), dma((6 * RING,)), dma((7,)), dma((7,)), dma((3,)), dma((3,)), dma((2,)),
    ]
    shapes = (
        jax.ShapeDtypeStruct((TOK, COLS), BF),
        jax.ShapeDtypeStruct((3, BLOCK, H), BF),
        jax.ShapeDtypeStruct((2, COLS, H), BF),
        jax.ShapeDtypeStruct((1, COLS, H), BF),
    )
    results = pl.pallas_call(
        kernel,
        out_shape=shapes,
        in_specs=[anywhere, anywhere, vmem, vmem, vmem, vmem],
        out_specs=(vmem, vmem, anywhere, anywhere),
        scratch_shapes=scratch,
        compiler_params=pltpu.CompilerParams(
            collective_id=0, has_side_effects=True, vmem_limit_bytes=58 * 1024 * 1024
        ),
        name="experts",
    )(
        expert_hidden,
        jnp.swapaxes(down_weight, 1, 2),
        out_grad,
        expert_ids.T,
        gate_code.T,
        expert_load.reshape(1, LANES),
    )
    mixed, hidden_grad, weight_grad, spare_grad = pl.pallas_call(
        store,
        out_shape=shapes,
        in_specs=[anywhere] * 4,
        out_specs=[anywhere] * 4,
        scratch_shapes=[b(TOK, COLS), b(3, BLOCK, H), b(2, COLS, H), b(1, COLS, H), dma((8,))],
        name="store",
    )(*results)
    return mixed, hidden_grad, jnp.swapaxes(weight_grad, 1, 2), jnp.swapaxes(spare_grad, 1, 2)


def solution(mesh):
    placed = (
        P("expert", None, None),
        P("expert", None, "dp"),
        P("expert", "dp"),
        P("expert", None),
        P("expert", None),
        P(),
    )
    return jax.shard_map(
        body,
        mesh=mesh,
        in_specs=placed,
        out_specs=(
            P("expert", "dp"),
            P("expert", "dp", None),
            P("expert", None, "dp"),
            P("expert", None, "dp"),
        ),
        check_vma=False,
    )
```

```python
import jax
import jax.numpy as jnp
from jax import lax
from jax.experimental import pallas as pl
from jax.experimental.pallas import tpu as pltpu
from jax.sharding import PartitionSpec as P

MESH = pl.DeviceIdType.MESH
BF = jnp.bfloat16
F32 = jnp.float32

Z = 8
X = 8
Y = 8
TOK = 96
LANES = 128
TOP = 8
MOST = 12
H = 1024
COLS = 224
HALF = 384
BLOCK = 48
RING = 7
SIDE = 512


def dot(a, b):
    return jnp.dot(a, b, preferred_element_type=F32)


def dot_nt(a, b):
    return lax.dot_general(a, b, (((1,), (1,)), ((), ())), preferred_element_type=F32)


def dot_tn(a, b):
    return lax.dot_general(a, b, (((0,), (0,)), ((), ())), preferred_element_type=F32)


def kernel(
    hid_hbm, w_hbm, og_ref, ids_ref, code_ref, load_ref,
    mixed_ref, hg_ref, wg_hbm, sg_hbm,
    hid, hid_n, hid_h, hid_c, w, w_n, w_h, w_c,
    meta, tok, perm, perm_h, perm_r,
    key_n, key_h, key_c, gate_n, gate_h, gate_c, g_n, g_hc, gt_n, gt_h, gt_c,
    out_n, out_h, out_c, send_n, send_hc, recv_n, recv_h, recv_c,
    sb_n, sb_h, sb_c, back_n, back_h, back_c, rg_n, rg_hc, rgt_n, rgt_hc,
    cxs_n, cxs_h, cxs_c, cxr_n, cxr_h, cxr_c, sum_n, sum_h, sum_c,
    rs_n, rs_h, rs_c, rr_n, rr_h, rr_c,
    mix_s, mix_r, mix_c, mixc_r, val_h, val_c, grad_h, wg, sg,
    load_sem, zt_s, zt_r, zm_s, zm_r, wc_s, wc_r,
    dn_s, dn_r, dh_s, dh_r, dc_s, dc_r, bn_s, bn_r, bh_s, bh_r, bc_s, bc_r,
    cx_s, cx_r, ring_s, ring_r, mx_s, mx_r, mxc_s, mxc_r, out_sem,
):
    e = lax.axis_index("expert")
    dp = lax.axis_index("dp")
    z, x, y, c = e // X, e % X, dp // 2, dp % 2
    h = z // 4

    def z_peer(d):
        return (((z + d) % Z) * X + x, dp)

    def x_peer(d):
        return (z * X + (x + d) % X, dp)

    def y_peer(d):
        return (e, ((y + d) % Y) * 2 + c)

    sibling = (e, y * 2 + 1 - c)

    def remote(src, dst, s, r, to):
        return pltpu.make_async_remote_copy(
            src_ref=src, dst_ref=dst, send_sem=s, recv_sem=r, device_id=to, device_id_type=MESH
        )

    loads = [
        pltpu.make_async_copy(w_hbm, w, load_sem.at[0]),
        pltpu.make_async_copy(hid_hbm.at[0], hid.at[0], load_sem.at[1]),
        pltpu.make_async_copy(hid_hbm.at[1], hid.at[1], load_sem.at[2]),
        pltpu.make_async_copy(
            hid_hbm.at[2, pl.ds(pl.multiple_of(h * HALF, HALF), HALF)], hid_c, load_sem.at[3]
        ),
    ]
    for copy in loads:
        copy.start()

    barrier = pltpu.get_barrier_semaphore()
    peers = [z_peer(d) for d in range(1, Z)] + [x_peer(d) for d in range(1, X)]
    peers += [y_peer(1), y_peer(-1), sibling]
    for peer in peers:
        pl.semaphore_signal(barrier, inc=1, device_id=peer, device_id_type=MESH)

    meta[z] = jnp.full((2 * TOP, LANES), -1.0, BF)
    facts = jnp.concatenate([ids_ref[...].astype(F32), code_ref[...].astype(F32)], axis=0)
    meta[z, :, 0:TOK] = facts.astype(BF)
    tok[z, 0:TOK] = og_ref[...]
    for i in range(Z):
        tok[i, TOK:LANES] = jnp.zeros((LANES - TOK, COLS), BF)

    pl.semaphore_wait(barrier, len(peers))

    near = [4 * h + (z + i) % 4 for i in range(1, 4)]
    far = [4 * (1 - h) + (z + i) % 4 for i in range(4)]
    gather = []
    for i, other in enumerate(near + far):
        peer = (other * X + x, dp)
        gather.append(remote(meta.at[z], meta.at[z], zm_s.at[i], zm_r.at[i], peer))
        gather.append(
            remote(tok.at[z, pl.ds(0, TOK)], tok.at[z, pl.ds(0, TOK)], zt_s.at[i], zt_r.at[i], peer)
        )
    for copy in gather:
        copy.start()

    lane = lax.broadcasted_iota(jnp.int32, (X, LANES), 1)
    at_x = lax.broadcasted_iota(jnp.int32, (X, 1), 0)
    loads_all = jnp.broadcast_to(load_ref[...].astype(F32), (X, LANES))

    def hottest(row_of_z):
        first = 2 * (row_of_z * X + at_x)
        even = jnp.sum(jnp.where(lane == first, loads_all, 0.0), axis=1, keepdims=True)
        odd = jnp.sum(jnp.where(lane == first + 1, loads_all, 0.0), axis=1, keepdims=True)
        return jnp.where(odd > even, 1.0, 0.0)

    hot_here = hottest(z)
    hot = jnp.sum(jnp.where(at_x == x, hot_here, 0.0), axis=0, keepdims=True)
    hot_b, cold_b = hot.astype(BF), (1.0 - hot).astype(BF)
    cold = 1.0 - hot

    loads[0].wait()
    w_h[...] = w[0] * cold_b + w[1] * hot_b
    w_n[...] = w[0] * hot_b + w[1] * cold_b

    row = lax.broadcasted_iota(jnp.int32, (TOK, 1), 0)
    outer = jnp.zeros((TOK, 1), jnp.int32)
    for k in range(1, 8):
        outer = outer + jnp.where(row >= k * MOST, 1, 0)
    moved = outer * TOK + row - outer * MOST
    col = lax.broadcasted_iota(jnp.int32, (TOK, 2 * HALF), 1)
    for k in range(8):
        perm[k * TOK : (k + 1) * TOK] = jnp.where(col == moved + k * MOST, 1.0, 0.0).astype(BF)
    for k in range(8):
        perm_h[k * BLOCK : (k + 1) * BLOCK] = perm[k * TOK : k * TOK + BLOCK, 0:HALF]
    perm_r[...] = perm_h[...].astype(F32).T.astype(BF)

    loads[1].wait()
    loads[2].wait()

    def forward_n(i, carry):
        at = pl.ds(pl.multiple_of(i * 256, 256), 256)
        rows = hid[0, at] * hot_b + hid[1, at] * cold_b
        hid_n[at] = rows
        out_n[at] = dot_nt(rows, w_n[...]).astype(BF)
        return carry

    lax.fori_loop(0, 3, forward_n, 0)
    back = []
    for i in range(2):
        part = dot(perm[i * HALF : (i + 1) * HALF], out_n[...]).astype(BF)
        sb_n[4 * i : 4 * i + 4] = part.reshape(4, TOK, COLS)
    for i, d in enumerate((4, 3, -3, 2, -2, 1, -1)):
        copy = remote(sb_n.at[(x + d) % X], back_n.at[(-d) % X], bn_s.at[i], bn_r.at[i], x_peer(d))
        copy.start()
        back.append(copy)
    back_n[0] = sb_n[x]

    for copy in gather[0:6]:
        copy.wait()
    spare = remote(w_h, w_c, wc_s.at[0], wc_r.at[0], z_peer(4))
    spare.start()

    far_z = (z + 4) % Z
    home = (2 * (z * X + at_x)).astype(F32)
    name_n = home + 1.0 - hot_here
    name_h = home + hot_here
    name_c = (2 * (far_z * X + at_x)).astype(F32) + hottest(far_z)
    before = jnp.where(
        lax.broadcasted_iota(jnp.int32, (LANES, LANES), 0) < lax.broadcasted_iota(jnp.int32, (LANES, LANES), 1), 1.0, 0.0
    ).astype(BF)

    def match(facts, name):
        hits = jnp.zeros((X, LANES), F32)
        gates = jnp.zeros((X, LANES), F32)
        for k in range(TOP):
            same = facts[k : k + 1, :] == name
            hits = hits + jnp.where(same, 1.0, 0.0)
            gates = gates + jnp.where(same, 0.0625 * (facts[TOP + k : TOP + k + 1, :] + 1.0), 0.0)
        return hits, gates

    def keys(hits, first):
        places = dot(hits.astype(BF), before)
        return jnp.where(hits > 0.5, places + first, -1.0)

    for i in range(4):
        facts = meta[4 * h + i].astype(F32)
        hits, gates = match(facts, name_h)
        key_h[:, i * LANES : (i + 1) * LANES] = keys(hits, float(i * MOST))
        gate_h[:, i * LANES : (i + 1) * LANES] = gates
        hits, gates = match(facts, name_c)
        key_c[:, i * LANES : (i + 1) * LANES] = keys(hits, float(BLOCK + i * MOST))
        gate_c[:, i * LANES : (i + 1) * LANES] = gates

    order = (0, 4, 3, 5, 2, 6, 1, 7)
    places_h = lax.broadcasted_iota(jnp.int32, (TOK, 4 * LANES), 0).astype(F32)
    dispatch_h = []
    for group in (order[0:4], order[4:8]):
        for d in group:
            at = pl.ds((x + d) % X, 1)
            i = order.index(d)
            g_hc[i * TOK : (i + 1) * TOK] = (
                jnp.where(key_h[at, :] == places_h, gate_h[at, :], 0.0)
                + jnp.where(key_c[at, :] == places_h, gate_c[at, :], 0.0)
            ).astype(BF)
        i = order.index(group[0])
        rows = dot(g_hc[i * TOK : (i + 4) * TOK], tok[pl.ds(4 * h, 4)].reshape(4 * LANES, COLS)).astype(BF)
        send_hc[i : i + 4] = rows.reshape(4, TOK, COLS)
        for d in group:
            i = order.index(d)
            if d:
                copy = remote(
                    send_hc.at[i, pl.ds(0, BLOCK)], recv_h.at[x], dh_s.at[i - 1], dh_r.at[i - 1], x_peer(d)
                )
                copy.start()
                dispatch_h.append(copy)
            else:
                recv_h[x] = send_hc[i, 0:BLOCK]
                recv_c[x] = send_hc[i, BLOCK:TOK]

    for copy in gather[6:]:
        copy.wait()
    for i in range(Z):
        hits, gates = match(meta[i].astype(F32), name_n)
        key_n[:, i * LANES : (i + 1) * LANES] = keys(hits, float(i * MOST))
        gate_n[:, i * LANES : (i + 1) * LANES] = gates
    places_n = lax.broadcasted_iota(jnp.int32, (TOK, Z * LANES), 0).astype(F32)
    dispatch_n = []
    for group in (order[0:4], order[4:8]):
        for d in group:
            at = pl.ds((x + d) % X, 1)
            i = order.index(d)
            g_n[i * TOK : (i + 1) * TOK] = jnp.where(key_n[at, :] == places_n, gate_n[at, :], 0.0).astype(BF)
        i = order.index(group[0])
        rows = dot(g_n[i * TOK : (i + 4) * TOK], tok[...].reshape(Z * LANES, COLS)).astype(BF)
        send_n[i : i + 4] = rows.reshape(4, TOK, COLS)
        for d in group:
            i = order.index(d)
            if d:
                copy = remote(send_n.at[i], recv_n.at[x], dn_s.at[i - 1], dn_r.at[i - 1], x_peer(d))
                copy.start()
                dispatch_n.append(copy)
            else:
                recv_n[x] = send_n[i]

    dispatch_c = []
    for i, d in enumerate(order):
        if d:
            copy = remote(
                send_hc.at[i, pl.ds(BLOCK, BLOCK)], recv_c.at[x], dc_s.at[i - 1], dc_r.at[i - 1], x_peer(d)
            )
            copy.start()
            dispatch_c.append(copy)

    def forward_h(i, carry):
        at = pl.ds(pl.multiple_of(i * 128, 128), 128)
        far = pl.ds(pl.multiple_of(h * HALF + i * 128, 128), 128)
        rows = hid[0, far] * cold_b + hid[1, far] * hot_b
        hid_h[at] = rows
        out_h[at] = dot_nt(rows, w_h[...]).astype(BF)
        return carry

    lax.fori_loop(0, 3, forward_h, 0)

    part = dot(perm_h[...], out_h[...]).astype(BF)
    sb_h[...] = part.reshape(X, BLOCK, COLS)
    for i in range(4):
        at = slice(i * 2 * LANES, (i + 1) * 2 * LANES)
        gt_n[at] = g_n[:, at].T
    for i in range(2):
        at = slice(i * 2 * LANES, (i + 1) * 2 * LANES)
        both = g_hc[:, at].reshape(X, TOK, 2 * LANES)
        gt_h[at] = both[:, 0:BLOCK].reshape(HALF, 2 * LANES).T
        gt_c[at] = both[:, BLOCK:TOK].reshape(HALF, 2 * LANES).T

    def partial(rg, first, count, weight, cxs, cxr, sums, sem):
        def rows_of(core):
            return jnp.concatenate(
                [
                    rg[pl.ds(pl.multiple_of(first + (2 * t + core) * BLOCK, 16), BLOCK), :]
                    for t in range(count)
                ],
                axis=0,
            )

        theirs = rows_of(1 - c)
        copies = []
        for side in range(2):
            part = dot(theirs, weight[:, side * SIDE : (side + 1) * SIDE]).astype(BF)
            cxs[side] = part.reshape(count, BLOCK, SIDE)
            copy = remote(cxs.at[side], cxr.at[side], cx_s.at[sem + side], cx_r.at[sem + side], sibling)
            copy.start()
            copies.append(copy)
        mine = rows_of(c)
        for side in range(2):
            part = dot(mine, weight[:, side * SIDE : (side + 1) * SIDE])
            sums[side] = part.reshape(count, BLOCK, SIDE)
        return copies

    def at_step(side, k):
        return (y - (1 - 2 * side) * (1 + k)) % Y

    def ring_copy(kind, side, k):
        rs, rr = ((rs_n, rr_n), (rs_h, rr_h), (rs_c, rr_c))[kind]
        i = (kind * 2 + side) * RING + k
        return remote(rs.at[side, k], rr.at[side, k], ring_s.at[i], ring_r.at[i], y_peer(1 - 2 * side))

    def block_sum(kind, side, t, k):
        sums, cxr, rr = ((sum_n, cxr_n, rr_n), (sum_h, cxr_h, rr_h), (sum_c, cxr_c, rr_c))[kind]
        total = sums[side, t] + cxr[side, t].astype(F32)
        if k > 0:
            total = total + rr[side, k - 1].astype(F32)
        return total

    def ring_step(kind, k):
        rs = (rs_n, rs_h, rs_c)[kind]
        for side in range(2):
            t = at_step(side, k)

            def go(side=side, t=t):
                if k > 0:
                    ring_copy(kind, side, k - 1).wait_recv()
                rs[side, k] = block_sum(kind, side, t if kind == 0 else t % 4, k).astype(BF)
                ring_copy(kind, side, k).start()

            if kind == 0:
                go()
            else:
                pl.when(t // 4 == h)(go)

    def ring_end(kind):
        for side in range(2):
            for k in range(RING):
                if kind == 0:
                    ring_copy(kind, side, k).wait_send()
                else:

                    @pl.when(at_step(side, k) // 4 == h)
                    def _(side=side, k=k):
                        ring_copy(kind, side, k).wait_send()

    for copy in dispatch_h:
        copy.wait()
    rg_hc[0:HALF] = dot(perm_r[...], recv_h[...].reshape(HALF, COLS)).astype(BF)
    pair_h = partial(rg_hc, 0, 4, w_h, cxs_h, cxr_h, sum_h, 2)
    for i, d in enumerate((4, 3, -3, 2, -2, 1, -1)):
        copy = remote(
            sb_h.at[(x + d) % X], back_h.at[order.index((-d) % X)], bh_s.at[i], bh_r.at[i], x_peer(d)
        )
        copy.start()
        back.append(copy)
    back_h[0] = sb_h[x]

    scale = 2.0 / TOK
    rgt_hc[:, 0:HALF] = rg_hc[0:HALF].T
    for i in range(2):
        at = slice(i * SIDE, (i + 1) * SIDE)
        grad_h[:, at] = scale * dot(rgt_hc[:, 0:HALF], hid_h[:, at])
    for copy in pair_h:
        copy.wait()
    ring_step(1, 0)

    for copy in back[0:7]:
        copy.wait()
    rows = jnp.concatenate([back_n[d] for d in order], axis=0)
    mix_s[...] = dot(gt_n[...], rows).reshape(Z, LANES, COLS)[:, 0:TOK]
    ring_step(1, 1)

    for copy in dispatch_n:
        copy.wait()
    for i in range(2):
        rows = dot(perm[i * HALF : (i + 1) * HALF], recv_n[...].reshape(2 * HALF, COLS)).astype(BF)
        rg_n[i * HALF : (i + 1) * HALF] = rows
    pair_n = partial(rg_n, 0, 8, w_n, cxs_n, cxr_n, sum_n, 0)
    ring_step(1, 2)

    for copy in pair_n:
        copy.wait()
    ring_step(0, 0)
    rgt_n[...] = rg_n[...].T
    ring_step(1, 3)
    ring_step(0, 1)

    def weight_part(i):
        at = slice(i * 256, (i + 1) * 256)
        grad_n = scale * dot(rgt_n[...], hid_n[:, at])
        wg[0, :, at] = (grad_n * hot + grad_h[:, at] * cold).astype(BF)
        wg[1, :, at] = (grad_n * cold + grad_h[:, at] * hot).astype(BF)

    def spare_part(i):
        at = slice(i * SIDE, (i + 1) * SIDE)
        sg[0, :, at] = (scale * dot(rgt_hc[:, HALF : 2 * HALF], hid_c[:, at])).astype(BF)

    weight_part(0)
    weight_part(1)
    ring_step(1, 4)
    ring_step(0, 2)

    spare.wait()
    loads[3].wait()

    def forward_c(i, carry):
        at = pl.ds(pl.multiple_of(i * 128, 128), 128)
        out_c[at] = dot_nt(hid_c[at], w_c[...]).astype(BF)
        return carry

    lax.fori_loop(0, 3, forward_c, 0)
    part = dot(perm_h[...], out_c[...]).astype(BF)
    sb_c[...] = part.reshape(X, BLOCK, COLS)
    for i, d in enumerate((4, 3, -3, 2, -2, 1, -1)):
        copy = remote(
            sb_c.at[(x + d) % X], back_c.at[order.index((-d) % X)], bc_s.at[i], bc_r.at[i], x_peer(d)
        )
        copy.start()
        back.append(copy)
    back_c[0] = sb_c[x]
    for copy in dispatch_c:
        copy.wait()
    rg_hc[HALF : 2 * HALF] = dot(perm_r[...], recv_c[...].reshape(HALF, COLS)).astype(BF)
    pair_c = partial(rg_hc, HALF, 4, w_c, cxs_c, cxr_c, sum_c, 4)
    ring_step(1, 5)
    ring_step(0, 3)
    rgt_hc[:, HALF : 2 * HALF] = rg_hc[HALF : 2 * HALF].T
    for copy in pair_c:
        copy.wait()
    ring_step(2, 0)
    ring_step(1, 6)
    ring_step(0, 4)

    for copy in back[7:14]:
        copy.wait()
    added = dot(gt_h[...], back_h[...].reshape(HALF, COLS)).reshape(4, LANES, COLS)
    mix_s[pl.ds(4 * h, 4)] = mix_s[pl.ds(4 * h, 4)] + added[:, 0:TOK]
    mix = []
    for i, other in enumerate(near + far):
        mix_r[8 + i] = mix_s[other].astype(BF)
        copy = remote(mix_r.at[8 + i], mix_r.at[i], mx_s.at[i], mx_r.at[i], (other * X + x, dp))
        copy.start()
        mix.append(copy)
    ring_step(2, 1)
    ring_step(0, 5)
    weight_part(2)
    ring_step(2, 2)
    ring_step(0, 6)
    weight_part(3)
    ring_step(2, 3)
    for copy in back[14:]:
        copy.wait()
    mix_c[...] = dot(gt_c[...], back_c[...].reshape(HALF, COLS)).reshape(4, LANES, COLS)[:, 0:TOK]
    for i, other in enumerate(near):
        mixc_r[4 + i] = mix_c[other % 4].astype(BF)
        copy = remote(mixc_r.at[4 + i], mixc_r.at[i], mxc_s.at[i], mxc_r.at[i], (other * X + x, dp))
        copy.start()
        mix.append(copy)
    ring_step(2, 4)
    spare_part(0)
    ring_step(2, 5)
    spare_part(1)
    stores = [
        pltpu.make_async_copy(wg, wg_hbm, out_sem.at[0]),
        pltpu.make_async_copy(sg, sg_hbm, out_sem.at[1]),
    ]
    for copy in stores:
        copy.start()
    ring_step(2, 6)

    val_h[...] = jnp.zeros_like(val_h)
    val_c[...] = jnp.zeros_like(val_c)
    value_n = []
    for side in range(2):
        ring_copy(0, side, RING - 1).wait_recv()
        value_n.append(block_sum(0, side, y, RING))

    @pl.when(y // 4 == h)
    def _():
        for side in range(2):
            at = slice(side * SIDE, (side + 1) * SIDE)
            ring_copy(1, side, RING - 1).wait_recv()
            val_h[:, at] = block_sum(1, side, y % 4, RING)
            ring_copy(2, side, RING - 1).wait_recv()
            val_c[:, at] = block_sum(2, side, y % 4, RING)

    for side in range(2):
        at = slice(side * SIDE, (side + 1) * SIDE)
        hg_ref[0, :, at] = (value_n[side] * hot + val_h[:, at] * cold).astype(BF)
        hg_ref[1, :, at] = (value_n[side] * cold + val_h[:, at] * hot).astype(BF)
    hg_ref[2] = val_c[...].astype(BF)

    total = mix_s[z] + mix_c[z % 4]
    for copy in mix:
        copy.wait()
    for i in range(Z - 1):
        total = total + mix_r[i].astype(F32)
    for i in range(3):
        total = total + mixc_r[i].astype(F32)
    mixed_ref[...] = total.astype(BF)

    for kind in range(3):
        ring_end(kind)
    for copy in stores:
        copy.wait()


def store(*refs):
    given, results, held, sem = refs[0:4], refs[4:8], refs[8:12], refs[12]
    inward = [pltpu.make_async_copy(given[i], held[i], sem.at[i]) for i in range(4)]
    outward = [pltpu.make_async_copy(held[i], results[i], sem.at[4 + i]) for i in range(4)]
    for i in range(4):
        inward[i].start()
    for i in range(4):
        inward[i].wait()
        outward[i].start()
    for i in range(4):
        outward[i].wait()


def body(expert_hidden, down_weight, out_grad, expert_ids, gate_code, expert_load):
    vmem = pl.BlockSpec(memory_space=pltpu.VMEM)
    anywhere = pl.BlockSpec(memory_space=pl.ANY)
    dma = pltpu.SemaphoreType.DMA

    def b(*shape):
        return pltpu.VMEM(shape, BF)

    def f(*shape):
        return pltpu.VMEM(shape, F32)

    scratch = [
        b(2, 2 * HALF, H), b(2 * HALF, H), b(HALF, H), b(HALF, H),
        b(2, COLS, H), b(COLS, H), b(COLS, H), b(COLS, H),
        b(Z, 2 * TOP, LANES), b(Z, LANES, COLS), b(2 * HALF, 2 * HALF), b(HALF, HALF), b(HALF, HALF),
        f(X, Z * LANES), f(X, 4 * LANES), f(X, 4 * LANES), f(X, Z * LANES), f(X, 4 * LANES), f(X, 4 * LANES),
        b(X * TOK, Z * LANES), b(X * TOK, 4 * LANES), b(Z * LANES, X * TOK), b(4 * LANES, HALF), b(4 * LANES, HALF),
        b(2 * HALF, COLS), b(HALF, COLS), b(HALF, COLS),
        b(X, TOK, COLS), b(X, TOK, COLS), b(X, TOK, COLS), b(X, BLOCK, COLS), b(X, BLOCK, COLS),
        b(X, TOK, COLS), b(X, BLOCK, COLS), b(X, BLOCK, COLS), b(X, TOK, COLS), b(X, BLOCK, COLS), b(X, BLOCK, COLS),
        b(2 * HALF, COLS), b(2 * HALF, COLS), b(COLS, 2 * HALF), b(COLS, 2 * HALF),
        b(2, 8, BLOCK, SIDE), b(2, 4, BLOCK, SIDE), b(2, 4, BLOCK, SIDE),
        b(2, 8, BLOCK, SIDE), b(2, 4, BLOCK, SIDE), b(2, 4, BLOCK, SIDE),
        f(2, 8, BLOCK, SIDE), f(2, 4, BLOCK, SIDE), f(2, 4, BLOCK, SIDE),
        b(2, RING, BLOCK, SIDE), b(2, RING, BLOCK, SIDE), b(2, RING, BLOCK, SIDE),
        b(2, RING, BLOCK, SIDE), b(2, RING, BLOCK, SIDE), b(2, RING, BLOCK, SIDE),
        f(Z, TOK, COLS), b(2 * Z, TOK, COLS), f(4, TOK, COLS), b(8, TOK, COLS), f(BLOCK, H), f(BLOCK, H), f(COLS, H), b(2, COLS, H), b(1, COLS, H),
        dma((4,)), dma((7,)), dma((7,)), dma((7,)), dma((7,)), dma((1,)), dma((1,)),
        dma((7,)), dma((7,)), dma((7,)), dma((7,)), dma((7,)), dma((7,)), dma((7,)), dma((7,)), dma((7,)), dma((7,)), dma((7,)), dma((7,)),
        dma((6,)), dma((6,)), dma((6 * RING,)), dma((6 * RING,)), dma((7,)), dma((7,)), dma((3,)), dma((3,)), dma((2,)),
    ]
    shapes = (
        jax.ShapeDtypeStruct((TOK, COLS), BF),
        jax.ShapeDtypeStruct((3, BLOCK, H), BF),
        jax.ShapeDtypeStruct((2, COLS, H), BF),
        jax.ShapeDtypeStruct((1, COLS, H), BF),
    )
    results = pl.pallas_call(
        kernel,
        out_shape=shapes,
        in_specs=[anywhere, anywhere, vmem, vmem, vmem, vmem],
        out_specs=(vmem, vmem, anywhere, anywhere),
        scratch_shapes=scratch,
        compiler_params=pltpu.CompilerParams(
            collective_id=0, has_side_effects=True, vmem_limit_bytes=58 * 1024 * 1024
        ),
        name="experts",
    )(
        expert_hidden,
        jnp.swapaxes(down_weight, 1, 2),
        out_grad,
        expert_ids.T,
        gate_code.T,
        expert_load.reshape(1, LANES),
    )
    mixed, hidden_grad, weight_grad, spare_grad = pl.pallas_call(
        store,
        out_shape=shapes,
        in_specs=[anywhere] * 4,
        out_specs=[anywhere] * 4,
        scratch_shapes=[b(TOK, COLS), b(3, BLOCK, H), b(2, COLS, H), b(1, COLS, H), dma((8,))],
        name="store",
    )(*results)
    return mixed, hidden_grad, jnp.swapaxes(weight_grad, 1, 2), jnp.swapaxes(spare_grad, 1, 2)


def solution(mesh):
    placed = (
        P("expert", None, None),
        P("expert", None, "dp"),
        P("expert", "dp"),
        P("expert", None),
        P("expert", None),
        P(),
    )
    return jax.shard_map(
        body,
        mesh=mesh,
        in_specs=placed,
        out_specs=(
            P("expert", "dp"),
            P("expert", "dp", None),
            P("expert", None, "dp"),
            P("expert", None, "dp"),
        ),
        check_vma=False,
    )
```

```python
import jax
import jax.numpy as jnp
from jax import lax
from jax.experimental import pallas as pl
from jax.experimental.pallas import tpu as pltpu
from jax.sharding import PartitionSpec as P

MESH = pl.DeviceIdType.MESH
BF = jnp.bfloat16
F32 = jnp.float32

Z = 8
X = 8
Y = 8
TOK = 96
LANES = 128
TOP = 8
MOST = 12
H = 1024
COLS = 224
HALF = 384
BLOCK = 48
RING = 7
SIDE = 512


def dot(a, b):
    return jnp.dot(a, b, preferred_element_type=F32)


def dot_nt(a, b):
    return lax.dot_general(a, b, (((1,), (1,)), ((), ())), preferred_element_type=F32)


def dot_tn(a, b):
    return lax.dot_general(a, b, (((0,), (0,)), ((), ())), preferred_element_type=F32)


def kernel(
    hid_hbm, w_hbm, og_ref, ids_ref, code_ref, load_ref,
    mixed_ref, hg_ref, wg_hbm, sg_hbm,
    hid, hid_n, hid_h, hid_c, w, w_n, w_h, w_c,
    meta, tok, perm, perm_h,
    key_n, key_h, key_c, gate_n, gate_h, gate_c, g_n, g_hc, gt_n, gt_h, gt_c,
    out_n, out_h, out_c, send_n, send_hc, recv_n, recv_hc,
    sb_n, sb_h, sb_c, back_n, back_h, back_c, rg_n, rg_hc, rgt_n, rgt_hc,
    cxs_n, cxs_h, cxs_c, cxr_n, cxr_h, cxr_c, sum_n, sum_h, sum_c,
    rs_n, rs_h, rs_c, rr_n, rr_h, rr_c,
    mix_s, mix_r, mix_c, mixc_r, val_h, val_c, grad_h, wg, sg,
    load_sem, zt_s, zt_r, zm_s, zm_r, wc_s, wc_r,
    dn_s, dn_r, dh_s, dh_r, bn_s, bn_r, bh_s, bh_r, bc_s, bc_r,
    cx_s, cx_r, ring_s, ring_r, mx_s, mx_r, mxc_s, mxc_r, out_sem,
):
    e = lax.axis_index("expert")
    dp = lax.axis_index("dp")
    z, x, y, c = e // X, e % X, dp // 2, dp % 2
    h = z // 4

    def z_peer(d):
        return (((z + d) % Z) * X + x, dp)

    def x_peer(d):
        return (z * X + (x + d) % X, dp)

    def y_peer(d):
        return (e, ((y + d) % Y) * 2 + c)

    sibling = (e, y * 2 + 1 - c)

    def remote(src, dst, s, r, to):
        return pltpu.make_async_remote_copy(
            src_ref=src, dst_ref=dst, send_sem=s, recv_sem=r, device_id=to, device_id_type=MESH
        )

    loads = [
        pltpu.make_async_copy(w_hbm, w, load_sem.at[0]),
        pltpu.make_async_copy(hid_hbm.at[0], hid.at[0], load_sem.at[1]),
        pltpu.make_async_copy(hid_hbm.at[1], hid.at[1], load_sem.at[2]),
        pltpu.make_async_copy(
            hid_hbm.at[2, pl.ds(pl.multiple_of(h * HALF, HALF), HALF)], hid_c, load_sem.at[3]
        ),
    ]
    for copy in loads:
        copy.start()

    barrier = pltpu.get_barrier_semaphore()
    peers = [z_peer(d) for d in range(1, Z)] + [x_peer(d) for d in range(1, X)]
    peers += [y_peer(1), y_peer(-1), sibling]
    for peer in peers:
        pl.semaphore_signal(barrier, inc=1, device_id=peer, device_id_type=MESH)

    meta[z] = jnp.full((2 * TOP, LANES), -1.0, BF)
    facts = jnp.concatenate([ids_ref[...].astype(F32), code_ref[...].astype(F32)], axis=0)
    meta[z, :, 0:TOK] = facts.astype(BF)
    tok[z, 0:TOK] = og_ref[...]
    for i in range(Z):
        tok[i, TOK:LANES] = jnp.zeros((LANES - TOK, COLS), BF)

    pl.semaphore_wait(barrier, len(peers))

    near = [4 * h + (z + i) % 4 for i in range(1, 4)]
    far = [4 * (1 - h) + (z + i) % 4 for i in range(4)]
    gather = []
    for i, other in enumerate(near + far):
        peer = (other * X + x, dp)
        gather.append(remote(meta.at[z], meta.at[z], zm_s.at[i], zm_r.at[i], peer))
        gather.append(
            remote(tok.at[z, pl.ds(0, TOK)], tok.at[z, pl.ds(0, TOK)], zt_s.at[i], zt_r.at[i], peer)
        )
    for copy in gather:
        copy.start()

    lane = lax.broadcasted_iota(jnp.int32, (X, LANES), 1)
    at_x = lax.broadcasted_iota(jnp.int32, (X, 1), 0)
    loads_all = jnp.broadcast_to(load_ref[...].astype(F32), (X, LANES))

    def hottest(row_of_z):
        first = 2 * (row_of_z * X + at_x)
        even = jnp.sum(jnp.where(lane == first, loads_all, 0.0), axis=1, keepdims=True)
        odd = jnp.sum(jnp.where(lane == first + 1, loads_all, 0.0), axis=1, keepdims=True)
        return jnp.where(odd > even, 1.0, 0.0)

    hot_here = hottest(z)
    hot = jnp.sum(jnp.where(at_x == x, hot_here, 0.0), axis=0, keepdims=True)
    hot_b, cold_b = hot.astype(BF), (1.0 - hot).astype(BF)
    cold = 1.0 - hot

    loads[0].wait()
    w_h[...] = w[0] * cold_b + w[1] * hot_b
    w_n[...] = w[0] * hot_b + w[1] * cold_b

    row = lax.broadcasted_iota(jnp.int32, (TOK, 1), 0)
    outer = jnp.zeros((TOK, 1), jnp.int32)
    for k in range(1, 8):
        outer = outer + jnp.where(row >= k * MOST, 1, 0)
    moved = outer * TOK + row - outer * MOST
    col = lax.broadcasted_iota(jnp.int32, (TOK, 2 * HALF), 1)
    for k in range(8):
        perm[k * TOK : (k + 1) * TOK] = jnp.where(col == moved + k * MOST, 1.0, 0.0).astype(BF)
    for k in range(8):
        perm_h[k * BLOCK : (k + 1) * BLOCK] = perm[k * TOK : k * TOK + BLOCK, 0:HALF]

    loads[1].wait()
    loads[2].wait()

    def forward_n(i, carry):
        at = pl.ds(pl.multiple_of(i * 256, 256), 256)
        rows = hid[0, at] * hot_b + hid[1, at] * cold_b
        hid_n[at] = rows
        out_n[at] = dot_nt(rows, w_n[...]).astype(BF)
        return carry

    lax.fori_loop(0, 3, forward_n, 0)
    back = []
    for i in range(2):
        part = dot(perm[i * HALF : (i + 1) * HALF], out_n[...]).astype(BF)
        sb_n[4 * i : 4 * i + 4] = part.reshape(4, TOK, COLS)
    for i, d in enumerate((4, 3, -3, 2, -2, 1, -1)):
        copy = remote(sb_n.at[(x + d) % X], back_n.at[(-d) % X], bn_s.at[i], bn_r.at[i], x_peer(d))
        copy.start()
        back.append(copy)
    back_n[0] = sb_n[x]

    for copy in gather[0:6]:
        copy.wait()
    spare = remote(w_h, w_c, wc_s.at[0], wc_r.at[0], z_peer(4))
    spare.start()

    far_z = (z + 4) % Z
    home = (2 * (z * X + at_x)).astype(F32)
    name_n = home + 1.0 - hot_here
    name_h = home + hot_here
    name_c = (2 * (far_z * X + at_x)).astype(F32) + hottest(far_z)
    before = jnp.where(
        lax.broadcasted_iota(jnp.int32, (LANES, LANES), 0) < lax.broadcasted_iota(jnp.int32, (LANES, LANES), 1), 1.0, 0.0
    ).astype(BF)

    def match(facts, name):
        hits = jnp.zeros((X, LANES), F32)
        gates = jnp.zeros((X, LANES), F32)
        for k in range(TOP):
            same = facts[k : k + 1, :] == name
            hits = hits + jnp.where(same, 1.0, 0.0)
            gates = gates + jnp.where(same, 0.0625 * (facts[TOP + k : TOP + k + 1, :] + 1.0), 0.0)
        return hits, gates

    def keys(hits, first):
        places = dot(hits.astype(BF), before)
        return jnp.where(hits > 0.5, places + first, -1.0)

    for i in range(4):
        facts = meta[4 * h + i].astype(F32)
        hits, gates = match(facts, name_h)
        key_h[:, i * LANES : (i + 1) * LANES] = keys(hits, float(i * MOST))
        gate_h[:, i * LANES : (i + 1) * LANES] = gates
        hits, gates = match(facts, name_c)
        key_c[:, i * LANES : (i + 1) * LANES] = keys(hits, float(BLOCK + i * MOST))
        gate_c[:, i * LANES : (i + 1) * LANES] = gates

    order = (0, 4, 3, 5, 2, 6, 1, 7)
    places_h = lax.broadcasted_iota(jnp.int32, (TOK, 4 * LANES), 0).astype(F32)
    dispatch_h = []
    for group in (order[0:4], order[4:8]):
        for d in group:
            at = pl.ds((x + d) % X, 1)
            i = order.index(d)
            g_hc[i * TOK : (i + 1) * TOK] = (
                jnp.where(key_h[at, :] == places_h, gate_h[at, :], 0.0)
                + jnp.where(key_c[at, :] == places_h, gate_c[at, :], 0.0)
            ).astype(BF)
        i = order.index(group[0])
        rows = dot(g_hc[i * TOK : (i + 4) * TOK], tok[pl.ds(4 * h, 4)].reshape(4 * LANES, COLS)).astype(BF)
        send_hc[i : i + 4] = rows.reshape(4, TOK, COLS)
        for d in group:
            i = order.index(d)
            if d:
                copy = remote(send_hc.at[i], recv_hc.at[x], dh_s.at[i - 1], dh_r.at[i - 1], x_peer(d))
                copy.start()
                dispatch_h.append(copy)
            else:
                recv_hc[x] = send_hc[i]

    for copy in gather[6:]:
        copy.wait()
    for i in range(Z):
        hits, gates = match(meta[i].astype(F32), name_n)
        key_n[:, i * LANES : (i + 1) * LANES] = keys(hits, float(i * MOST))
        gate_n[:, i * LANES : (i + 1) * LANES] = gates
    places_n = lax.broadcasted_iota(jnp.int32, (TOK, Z * LANES), 0).astype(F32)
    dispatch_n = []
    for group in (order[0:4], order[4:8]):
        for d in group:
            at = pl.ds((x + d) % X, 1)
            i = order.index(d)
            g_n[i * TOK : (i + 1) * TOK] = jnp.where(key_n[at, :] == places_n, gate_n[at, :], 0.0).astype(BF)
        i = order.index(group[0])
        rows = dot(g_n[i * TOK : (i + 4) * TOK], tok[...].reshape(Z * LANES, COLS)).astype(BF)
        send_n[i : i + 4] = rows.reshape(4, TOK, COLS)
        for d in group:
            i = order.index(d)
            if d:
                copy = remote(send_n.at[i], recv_n.at[x], dn_s.at[i - 1], dn_r.at[i - 1], x_peer(d))
                copy.start()
                dispatch_n.append(copy)
            else:
                recv_n[x] = send_n[i]

    def forward_h(i, carry):
        at = pl.ds(pl.multiple_of(i * 128, 128), 128)
        far = pl.ds(pl.multiple_of(h * HALF + i * 128, 128), 128)
        rows = hid[0, far] * cold_b + hid[1, far] * hot_b
        hid_h[at] = rows
        out_h[at] = dot_nt(rows, w_h[...]).astype(BF)
        return carry

    lax.fori_loop(0, 3, forward_h, 0)

    part = dot(perm_h[...], out_h[...]).astype(BF)
    sb_h[...] = part.reshape(X, BLOCK, COLS)
    for i in range(4):
        at = slice(i * 2 * LANES, (i + 1) * 2 * LANES)
        gt_n[at] = g_n[:, at].T
    for i in range(2):
        at = slice(i * 2 * LANES, (i + 1) * 2 * LANES)
        both = g_hc[:, at].reshape(X, TOK, 2 * LANES)
        gt_h[at] = both[:, 0:BLOCK].reshape(HALF, 2 * LANES).T
        gt_c[at] = both[:, BLOCK:TOK].reshape(HALF, 2 * LANES).T

    def partial(rg, first, count, weight, cxs, cxr, sums, sem):
        def rows_of(core):
            return jnp.concatenate(
                [
                    rg[pl.ds(pl.multiple_of(first + (2 * t + core) * BLOCK, 16), BLOCK), :]
                    for t in range(count)
                ],
                axis=0,
            )

        theirs = rows_of(1 - c)
        copies = []
        for side in range(2):
            part = dot(theirs, weight[:, side * SIDE : (side + 1) * SIDE]).astype(BF)
            cxs[side] = part.reshape(count, BLOCK, SIDE)
            copy = remote(cxs.at[side], cxr.at[side], cx_s.at[sem + side], cx_r.at[sem + side], sibling)
            copy.start()
            copies.append(copy)
        mine = rows_of(c)
        for side in range(2):
            part = dot(mine, weight[:, side * SIDE : (side + 1) * SIDE])
            sums[side] = part.reshape(count, BLOCK, SIDE)
        return copies

    def at_step(side, k):
        return (y - (1 - 2 * side) * (1 + k)) % Y

    def ring_copy(kind, side, k):
        rs, rr = ((rs_n, rr_n), (rs_h, rr_h), (rs_c, rr_c))[kind]
        i = (kind * 2 + side) * RING + k
        return remote(rs.at[side, k], rr.at[side, k], ring_s.at[i], ring_r.at[i], y_peer(1 - 2 * side))

    def block_sum(kind, side, t, k):
        sums, cxr, rr = ((sum_n, cxr_n, rr_n), (sum_h, cxr_h, rr_h), (sum_c, cxr_c, rr_c))[kind]
        total = sums[side, t] + cxr[side, t].astype(F32)
        if k > 0:
            total = total + rr[side, k - 1].astype(F32)
        return total

    def ring_step(kind, k):
        rs = (rs_n, rs_h, rs_c)[kind]
        for side in range(2):
            t = at_step(side, k)

            def go(side=side, t=t):
                if k > 0:
                    ring_copy(kind, side, k - 1).wait_recv()
                rs[side, k] = block_sum(kind, side, t if kind == 0 else t % 4, k).astype(BF)
                ring_copy(kind, side, k).start()

            if kind == 0:
                go()
            else:
                pl.when(t // 4 == h)(go)

    def ring_end(kind):
        for side in range(2):
            for k in range(RING):
                if kind == 0:
                    ring_copy(kind, side, k).wait_send()
                else:

                    @pl.when(at_step(side, k) // 4 == h)
                    def _(side=side, k=k):
                        ring_copy(kind, side, k).wait_send()

    for copy in dispatch_h:
        copy.wait()
    for i in range(2):
        rows = dot(perm[i * HALF : (i + 1) * HALF], recv_hc[...].reshape(2 * HALF, COLS)).astype(BF)
        rg_hc[i * HALF : (i + 1) * HALF] = rows
    pair_h = partial(rg_hc, 0, 4, w_h, cxs_h, cxr_h, sum_h, 2)
    for i, d in enumerate((4, 3, -3, 2, -2, 1, -1)):
        copy = remote(
            sb_h.at[(x + d) % X], back_h.at[order.index((-d) % X)], bh_s.at[i], bh_r.at[i], x_peer(d)
        )
        copy.start()
        back.append(copy)
    back_h[0] = sb_h[x]

    scale = 2.0 / TOK
    loads[3].wait()
    rgt_hc[...] = rg_hc[...].T
    for i in range(2):
        at = slice(i * SIDE, (i + 1) * SIDE)
        grad_h[:, at] = scale * dot(rgt_hc[:, 0:HALF], hid_h[:, at])
        sg[0, :, at] = (scale * dot(rgt_hc[:, HALF : 2 * HALF], hid_c[:, at])).astype(BF)
    for copy in pair_h:
        copy.wait()
    ring_step(1, 0)

    for copy in back[0:7]:
        copy.wait()
    rows = jnp.concatenate([back_n[d] for d in order], axis=0)
    mix_s[...] = dot(gt_n[...], rows).reshape(Z, LANES, COLS)[:, 0:TOK]
    ring_step(1, 1)

    for copy in dispatch_n:
        copy.wait()
    for i in range(2):
        rows = dot(perm[i * HALF : (i + 1) * HALF], recv_n[...].reshape(2 * HALF, COLS)).astype(BF)
        rg_n[i * HALF : (i + 1) * HALF] = rows
    pair_n = partial(rg_n, 0, 8, w_n, cxs_n, cxr_n, sum_n, 0)
    ring_step(1, 2)

    spare.wait()

    def forward_c(i, carry):
        at = pl.ds(pl.multiple_of(i * 128, 128), 128)
        out_c[at] = dot_nt(hid_c[at], w_c[...]).astype(BF)
        return carry

    lax.fori_loop(0, 3, forward_c, 0)
    part = dot(perm_h[...], out_c[...]).astype(BF)
    sb_c[...] = part.reshape(X, BLOCK, COLS)
    for i, d in enumerate((4, 3, -3, 2, -2, 1, -1)):
        copy = remote(
            sb_c.at[(x + d) % X], back_c.at[order.index((-d) % X)], bc_s.at[i], bc_r.at[i], x_peer(d)
        )
        copy.start()
        back.append(copy)
    back_c[0] = sb_c[x]
    for copy in pair_n:
        copy.wait()
    ring_step(0, 0)
    pair_c = partial(rg_hc, HALF, 4, w_c, cxs_c, cxr_c, sum_c, 4)
    ring_step(1, 3)
    ring_step(0, 1)
    for copy in pair_c:
        copy.wait()
    ring_step(2, 0)

    def weight_part(i):
        at = slice(i * 256, (i + 1) * 256)
        grad_n = scale * dot(rgt_n[...], hid_n[:, at])
        wg[0, :, at] = (grad_n * hot + grad_h[:, at] * cold).astype(BF)
        wg[1, :, at] = (grad_n * cold + grad_h[:, at] * hot).astype(BF)

    rgt_n[...] = rg_n[...].T
    ring_step(1, 4)
    ring_step(0, 2)
    ring_step(2, 1)

    for copy in back[7:14]:
        copy.wait()
    added = dot(gt_h[...], back_h[...].reshape(HALF, COLS)).reshape(4, LANES, COLS)
    mix_s[pl.ds(4 * h, 4)] = mix_s[pl.ds(4 * h, 4)] + added[:, 0:TOK]
    mix = []
    for i, other in enumerate(near + far):
        mix_r[8 + i] = mix_s[other].astype(BF)
        copy = remote(mix_r.at[8 + i], mix_r.at[i], mx_s.at[i], mx_r.at[i], (other * X + x, dp))
        copy.start()
        mix.append(copy)
    ring_step(1, 5)
    ring_step(0, 3)
    ring_step(2, 2)
    weight_part(0)
    ring_step(1, 6)
    ring_step(0, 4)
    ring_step(2, 3)
    for copy in back[14:]:
        copy.wait()
    mix_c[...] = dot(gt_c[...], back_c[...].reshape(HALF, COLS)).reshape(4, LANES, COLS)[:, 0:TOK]
    for i, other in enumerate(near):
        mixc_r[4 + i] = mix_c[other % 4].astype(BF)
        copy = remote(mixc_r.at[4 + i], mixc_r.at[i], mxc_s.at[i], mxc_r.at[i], (other * X + x, dp))
        copy.start()
        mix.append(copy)
    ring_step(0, 5)
    ring_step(2, 4)
    weight_part(1)
    ring_step(0, 6)
    ring_step(2, 5)
    weight_part(2)
    ring_step(2, 6)
    weight_part(3)
    stores = [
        pltpu.make_async_copy(wg, wg_hbm, out_sem.at[0]),
        pltpu.make_async_copy(sg, sg_hbm, out_sem.at[1]),
    ]
    for copy in stores:
        copy.start()

    val_h[...] = jnp.zeros_like(val_h)
    val_c[...] = jnp.zeros_like(val_c)
    value_n = []
    for side in range(2):
        ring_copy(0, side, RING - 1).wait_recv()
        value_n.append(block_sum(0, side, y, RING))

    @pl.when(y // 4 == h)
    def _():
        for side in range(2):
            at = slice(side * SIDE, (side + 1) * SIDE)
            ring_copy(1, side, RING - 1).wait_recv()
            val_h[:, at] = block_sum(1, side, y % 4, RING)
            ring_copy(2, side, RING - 1).wait_recv()
            val_c[:, at] = block_sum(2, side, y % 4, RING)

    for side in range(2):
        at = slice(side * SIDE, (side + 1) * SIDE)
        hg_ref[0, :, at] = (value_n[side] * hot + val_h[:, at] * cold).astype(BF)
        hg_ref[1, :, at] = (value_n[side] * cold + val_h[:, at] * hot).astype(BF)
    hg_ref[2] = val_c[...].astype(BF)

    total = mix_s[z] + mix_c[z % 4]
    for copy in mix:
        copy.wait()
    for i in range(Z - 1):
        total = total + mix_r[i].astype(F32)
    for i in range(3):
        total = total + mixc_r[i].astype(F32)
    mixed_ref[...] = total.astype(BF)

    for kind in range(3):
        ring_end(kind)
    for copy in stores:
        copy.wait()


def store(*refs):
    given, results, held, sem = refs[0:4], refs[4:8], refs[8:12], refs[12]
    inward = [pltpu.make_async_copy(given[i], held[i], sem.at[i]) for i in range(4)]
    outward = [pltpu.make_async_copy(held[i], results[i], sem.at[4 + i]) for i in range(4)]
    for i in range(4):
        inward[i].start()
    for i in range(4):
        inward[i].wait()
        outward[i].start()
    for i in range(4):
        outward[i].wait()


def body(expert_hidden, down_weight, out_grad, expert_ids, gate_code, expert_load):
    vmem = pl.BlockSpec(memory_space=pltpu.VMEM)
    anywhere = pl.BlockSpec(memory_space=pl.ANY)
    dma = pltpu.SemaphoreType.DMA

    def b(*shape):
        return pltpu.VMEM(shape, BF)

    def f(*shape):
        return pltpu.VMEM(shape, F32)

    scratch = [
        b(2, 2 * HALF, H), b(2 * HALF, H), b(HALF, H), b(HALF, H),
        b(2, COLS, H), b(COLS, H), b(COLS, H), b(COLS, H),
        b(Z, 2 * TOP, LANES), b(Z, LANES, COLS), b(2 * HALF, 2 * HALF), b(HALF, HALF),
        f(X, Z * LANES), f(X, 4 * LANES), f(X, 4 * LANES), f(X, Z * LANES), f(X, 4 * LANES), f(X, 4 * LANES),
        b(X * TOK, Z * LANES), b(X * TOK, 4 * LANES), b(Z * LANES, X * TOK), b(4 * LANES, HALF), b(4 * LANES, HALF),
        b(2 * HALF, COLS), b(HALF, COLS), b(HALF, COLS),
        b(X, TOK, COLS), b(X, TOK, COLS), b(X, TOK, COLS), b(X, TOK, COLS),
        b(X, TOK, COLS), b(X, BLOCK, COLS), b(X, BLOCK, COLS), b(X, TOK, COLS), b(X, BLOCK, COLS), b(X, BLOCK, COLS),
        b(2 * HALF, COLS), b(2 * HALF, COLS), b(COLS, 2 * HALF), b(COLS, 2 * HALF),
        b(2, 8, BLOCK, SIDE), b(2, 4, BLOCK, SIDE), b(2, 4, BLOCK, SIDE),
        b(2, 8, BLOCK, SIDE), b(2, 4, BLOCK, SIDE), b(2, 4, BLOCK, SIDE),
        f(2, 8, BLOCK, SIDE), f(2, 4, BLOCK, SIDE), f(2, 4, BLOCK, SIDE),
        b(2, RING, BLOCK, SIDE), b(2, RING, BLOCK, SIDE), b(2, RING, BLOCK, SIDE),
        b(2, RING, BLOCK, SIDE), b(2, RING, BLOCK, SIDE), b(2, RING, BLOCK, SIDE),
        f(Z, TOK, COLS), b(2 * Z, TOK, COLS), f(4, TOK, COLS), b(8, TOK, COLS), f(BLOCK, H), f(BLOCK, H), f(COLS, H), b(2, COLS, H), b(1, COLS, H),
        dma((4,)), dma((7,)), dma((7,)), dma((7,)), dma((7,)), dma((1,)), dma((1,)),
        dma((7,)), dma((7,)), dma((7,)), dma((7,)), dma((7,)), dma((7,)), dma((7,)), dma((7,)), dma((7,)), dma((7,)),
        dma((6,)), dma((6,)), dma((6 * RING,)), dma((6 * RING,)), dma((7,)), dma((7,)), dma((3,)), dma((3,)), dma((2,)),
    ]
    shapes = (
        jax.ShapeDtypeStruct((TOK, COLS), BF),
        jax.ShapeDtypeStruct((3, BLOCK, H), BF),
        jax.ShapeDtypeStruct((2, COLS, H), BF),
        jax.ShapeDtypeStruct((1, COLS, H), BF),
    )
    results = pl.pallas_call(
        kernel,
        out_shape=shapes,
        in_specs=[anywhere, anywhere, vmem, vmem, vmem, vmem],
        out_specs=(vmem, vmem, anywhere, anywhere),
        scratch_shapes=scratch,
        compiler_params=pltpu.CompilerParams(
            collective_id=0, has_side_effects=True, vmem_limit_bytes=58 * 1024 * 1024
        ),
        name="experts",
    )(
        expert_hidden,
        jnp.swapaxes(down_weight, 1, 2),
        out_grad,
        expert_ids.T,
        gate_code.T,
        expert_load.reshape(1, LANES),
    )
    mixed, hidden_grad, weight_grad, spare_grad = pl.pallas_call(
        store,
        out_shape=shapes,
        in_specs=[anywhere] * 4,
        out_specs=[anywhere] * 4,
        scratch_shapes=[b(TOK, COLS), b(3, BLOCK, H), b(2, COLS, H), b(1, COLS, H), dma((8,))],
        name="store",
    )(*results)
    return mixed, hidden_grad, jnp.swapaxes(weight_grad, 1, 2), jnp.swapaxes(spare_grad, 1, 2)


def solution(mesh):
    placed = (
        P("expert", None, None),
        P("expert", None, "dp"),
        P("expert", "dp"),
        P("expert", None),
        P("expert", None),
        P(),
    )
    return jax.shard_map(
        body,
        mesh=mesh,
        in_specs=placed,
        out_specs=(
            P("expert", "dp"),
            P("expert", "dp", None),
            P("expert", None, "dp"),
            P("expert", None, "dp"),
        ),
        check_vma=False,
    )
```
